512 devices in a mesh: rows: 16 (over z_lo, y), cols: 32 (over z_hi, x, core).
Axes of the slice: x: 4, y: 4, z: 16 (z_hi: 4, z_lo: 4; z = z_hi * 4 + z_lo), core: 2. Of those that a mesh axis runs over, the one named last changes fastest.
Arguments:
- iterate: bfloat16 [3584, 18432], P('rows', 'cols'), may hold values from -1 to 1, as said below
Outputs:
- update: bfloat16 [3584, 18432], P('rows', 'cols')
The draws below stay inside these ranges and needn't reach their ends.
Inputs may be any that keep to these rules, and one draw needn't show every extreme that they name: `iterate`: entries are of size about 1/sqrt(18432) times a row scale between 0.6 and 1.3; no further structure is promised.
All inputs are finite; a program needn't handle non-finite values.
Results may differ from the reference program's by a relative error of at most 0.029.
Values may be sent and summed in bfloat16 or wider, within the bound.
No kernel may reach another device: no remote copies, remote signals or barrier semaphores. Data moves between devices by JAX's collectives and lax.ppermute only.
A program may use at most 64 MiB of HBM per device.

```python
import math
import jax
import jax.numpy as jnp

D = 3584
FF = 18432


def draw_iterate(key, part):
    key = jax.random.fold_in(key, 11)
    first, second = jax.random.split(key)
    base = jax.random.truncated_normal(first, -4.0, 4.0, (D, FF), jnp.float32)
    scales = jax.random.uniform(second, (D, 1), jnp.float32, 0.7, 1.3)
    return (base * scales * (1.0 / math.sqrt(FF))).astype(jnp.bfloat16)


def setup_inputs(seed: int = 0) -> dict:
    streams_of = jax.random.split(jax.random.key(seed), 2)
    return {
        "iterate": draw_iterate(jax.random.fold_in(streams_of[1], 71), 0),
    }


coef_linear = 3.4445
coef_cubic = -4.775
coef_quintic = 2.0315

def reference(iterate):
    gram = jnp.dot(iterate, iterate.T, preferred_element_type=jnp.float32).astype(jnp.bfloat16)
    square = jnp.dot(gram, gram, preferred_element_type=jnp.float32)
    poly = (coef_cubic * gram.astype(jnp.float32) + coef_quintic * square).astype(jnp.bfloat16)
    step = coef_linear * iterate.astype(jnp.float32) + jnp.dot(poly, iterate, preferred_element_type=jnp.float32)
    return (0.2 * math.sqrt(max(D, FF)) * step).astype(jnp.bfloat16)
```

```python
import math

import jax
import jax.numpy as jnp
from jax import lax
from jax.sharding import Mesh
from jax.sharding import PartitionSpec as P

D = 3584
FF = 18432

coef_linear = 3.4445
coef_cubic = -4.775
coef_quintic = 2.0315

SWAP = [(0, 1), (1, 0)]


def product(lhs, rhs, contract):
    return lax.dot_general(
        lhs, rhs, ((contract[:1], contract[1:]), ((), ())), preferred_element_type=jnp.float32
    )


def total(parts):
    return jnp.sum(parts.astype(jnp.float32), axis=0)


def shards(iterate):
    core = lax.axis_index("core")
    rows, cols = iterate.shape
    left = lax.all_gather(iterate, "y", axis=0).reshape(4 * rows, cols)
    right = lax.all_gather(iterate, "z_lo", axis=0).reshape(4 * rows, cols)

    tile = product(left, right, (1, 1)).astype(jnp.bfloat16).reshape(2, 2 * rows, 4 * rows)
    away = lax.dynamic_index_in_dim(tile, 1 - core, 0, keepdims=False)
    kept = lax.dynamic_index_in_dim(tile, core, 0, keepdims=False)
    half = kept.astype(jnp.float32) + lax.ppermute(away, "core", SWAP).astype(jnp.float32)
    pieces = half.astype(jnp.bfloat16).reshape(4, rows // 2, 4 * rows)
    piece = total(lax.all_to_all(pieces, "x", 0, 0, tiled=True)).astype(jnp.bfloat16)
    piece = total(lax.all_gather(piece, "z_hi", axis=0)).astype(jnp.bfloat16)
    mine = lax.all_gather(piece, "x", axis=0).reshape(2 * rows, 4 * rows)
    other = lax.ppermute(mine, "core", SWAP)
    gram = jnp.concatenate(
        [jnp.where(core == 0, mine, other), jnp.where(core == 0, other, mine)], axis=0
    )

    once = product(gram, right, (1, 0)).astype(jnp.bfloat16).reshape(4, rows, cols)
    once = total(lax.all_to_all(once, "y", 0, 0, tiled=True))
    ours = lax.all_gather(once.astype(jnp.bfloat16), "y", axis=0).reshape(4 * rows, cols)
    twice = product(gram, ours, (0, 0)).astype(jnp.bfloat16).reshape(4, rows, cols)
    twice = total(lax.all_to_all(twice, "z_lo", 0, 0, tiled=True))

    step = coef_linear * iterate.astype(jnp.float32) + coef_cubic * once + coef_quintic * twice
    return (0.2 * math.sqrt(max(D, FF)) * step).astype(jnp.bfloat16)


def solution(mesh):
    axes = ("z_lo", "y", "z_hi", "x", "core")
    fine = Mesh(mesh.devices.reshape(4, 4, 4, 4, 2), axes)
    placed = P(axes[:2], axes[2:])
    return jax.shard_map(
        shards, mesh=fine, in_specs=(placed,), out_specs=placed, check_vma=False
    )
```

```python
import math

import jax
import jax.numpy as jnp
from jax import lax
from jax.sharding import Mesh
from jax.sharding import PartitionSpec as P

D = 3584
FF = 18432

coef_linear = 3.4445
coef_cubic = -4.775
coef_quintic = 2.0315

SWAP = [(0, 1), (1, 0)]

SAME_Y = [[4 * y + (s - y) % 4 for s in range(4)] for y in range(4)]
SAME_X = [[4 * ((s - x) % 4) + x for s in range(4)] for x in range(4)]
SAME_S = [[4 * y + (s - y) % 4 for y in range(4)] for s in range(4)]
SAME_Y_CORES = [[2 * i + core for i in group for core in range(2)] for group in SAME_Y]


def product(lhs, rhs, contract):
    return lax.dot_general(
        lhs, rhs, ((contract[:1], contract[1:]), ((), ())), preferred_element_type=jnp.float32
    )


def total(parts):
    return jnp.sum(parts.astype(jnp.float32), axis=0)


def shards(iterate):
    core = lax.axis_index("core")
    rows, cols = iterate.shape
    right = lax.all_gather(iterate, "z_lo", axis=0).reshape(4 * rows, cols)
    left = lax.all_gather(iterate, "y", axis=0).reshape(4 * rows, cols)
    whole = lax.all_gather(right, "y", axis=0).reshape(16 * rows, cols)

    tile = product(left, right, (1, 1)).astype(jnp.bfloat16).reshape(4, 2, rows // 2, 4 * rows)
    away = lax.dynamic_index_in_dim(tile, 1 - core, 1, keepdims=False)
    kept = lax.dynamic_index_in_dim(tile, core, 1, keepdims=False)
    half = kept.astype(jnp.float32) + lax.ppermute(away, "core", SWAP).astype(jnp.float32)
    half = lax.all_to_all(
        half.astype(jnp.bfloat16), ("y", "x"), 0, 0, tiled=True, axis_index_groups=SAME_Y
    )
    piece = total(half).astype(jnp.bfloat16)
    piece = total(lax.all_gather(piece, "z_hi", axis=0)).astype(jnp.bfloat16)

    mine = lax.all_gather(piece, ("y", "x"), axis=0, axis_index_groups=SAME_S)
    other = lax.ppermute(mine, "core", SWAP)
    gram = lax.all_gather(piece, ("y", "x", "core"), axis=0, axis_index_groups=SAME_Y_CORES)
    gram = gram.reshape(4 * rows, 4 * rows)
    band = jnp.stack([jnp.where(core == 0, mine, other), jnp.where(core == 0, other, mine)], axis=0)
    band = band.transpose(0, 2, 1, 3).reshape(rows, 16 * rows)

    once = product(band, whole, (1, 0)).astype(jnp.bfloat16)
    once = lax.all_gather(once, ("y", "x"), axis=0, axis_index_groups=SAME_X)
    twice = product(gram, once.reshape(4 * rows, cols), (0, 0))
    twice = twice.astype(jnp.bfloat16).reshape(4, rows, cols)
    twice = total(lax.all_to_all(twice, "z_lo", 0, 0, tiled=True))
    once = lax.dynamic_index_in_dim(once, lax.axis_index("y"), 0, keepdims=False)

    step = coef_linear * iterate.astype(jnp.float32) + coef_cubic * once.astype(jnp.float32)
    step = step + coef_quintic * twice
    return (0.2 * math.sqrt(max(D, FF)) * step).astype(jnp.bfloat16)


def solution(mesh):
    axes = ("z_lo", "y", "z_hi", "x", "core")
    fine = Mesh(mesh.devices.reshape(4, 4, 4, 4, 2), axes)
    placed = P(axes[:2], axes[2:])
    return jax.shard_map(
        shards, mesh=fine, in_specs=(placed,), out_specs=placed, check_vma=False
    )
```

```python
import functools
import math

import jax
import jax.numpy as jnp
from jax import lax
from jax.experimental import pallas as pl
from jax.experimental.pallas import tpu as pltpu
from jax.sharding import Mesh
from jax.sharding import PartitionSpec as P

D = 3584
FF = 18432

coef_linear = 3.4445
coef_cubic = -4.775
coef_quintic = 2.0315

SWAP = [(0, 1), (1, 0)]
VMEM = pl.BlockSpec(memory_space=pltpu.VMEM)
SMEM = pl.BlockSpec(memory_space=pltpu.SMEM)


def call(kernel, shape, in_specs, flops):
    size = 2 * math.prod(shape)
    return pl.pallas_call(
        kernel,
        out_shape=jax.ShapeDtypeStruct(shape, jnp.bfloat16),
        in_specs=in_specs,
        out_specs=VMEM,
        compiler_params=pltpu.CompilerParams(vmem_limit_bytes=32 * 1024 * 1024),
        cost_estimate=pl.CostEstimate(flops=flops, bytes_accessed=4 * size, transcendentals=0),
    )


def dot(lhs, rhs, rhs_dim):
    return lax.dot_general(
        lhs, rhs, (((1,), (rhs_dim,)), ((), ())), preferred_element_type=jnp.float32
    )


def gram_kernel(left, right, right_other, out):
    blocks, _, rows, cols = left.shape
    tile = dot(left[:, 0].reshape(blocks * rows, cols), right[...], 1)
    tile += dot(left[:, 1].reshape(blocks * rows, cols), right_other[...], 1)
    out[...] = tile.astype(out.dtype).reshape(out.shape)


def product_kernel(core, mine, other, right, out):
    blocks, rows, inner = mine.shape
    for half, place in ((mine, core[0]), (other, 1 - core[0])):
        half = dot(half[...].reshape(blocks * rows, inner), right[...], 0)
        half = half.astype(out.dtype).reshape(blocks, 1, rows, out.shape[-1])
        out[:, pl.ds(place, 1)] = half


def total(parts):
    return jnp.sum(parts.astype(jnp.float32), axis=0)


def shards(iterate):
    core = lax.axis_index("core")
    rows, cols = iterate.shape
    half = rows // 2
    halves = iterate.reshape(2, half, cols)
    away = lax.dynamic_index_in_dim(halves, 1 - core, 0, keepdims=False)
    kept = lax.dynamic_index_in_dim(halves, core, 0, keepdims=False)
    kept = jnp.stack([kept, lax.ppermute(away, "core", SWAP)])
    right = lax.all_gather(iterate, "z_lo", axis=0).reshape(4 * rows, cols)
    right_other = lax.ppermute(right, "core", SWAP)
    left = lax.all_gather(kept, "y", axis=0)

    tile = call(gram_kernel, (4, half, 4 * rows), [VMEM] * 3, 2 * 4 * half * 4 * rows * 2 * cols)(
        left, right, right_other
    )
    piece = total(lax.all_to_all(tile, "x", 0, 0, tiled=True)).astype(jnp.bfloat16)
    piece = total(lax.all_gather(piece, "z_hi", axis=0)).astype(jnp.bfloat16)
    mine = lax.all_gather(piece, "x", axis=0)
    other = lax.ppermute(mine, "core", SWAP)

    multiply = call(
        product_kernel,
        (4, 2, half, cols),
        [SMEM] + [VMEM] * 3,
        2 * 4 * rows * 4 * rows * cols,
    )
    multiply = functools.partial(multiply, core.astype(jnp.int32).reshape(1), mine, other)

    def gram_times(array):
        parts = multiply(array).reshape(4, rows, cols)
        return total(lax.all_to_all(parts, "y", 0, 0, tiled=True))

    once = gram_times(right)
    gathered = lax.all_gather(once.astype(jnp.bfloat16), "z_lo", axis=0)
    twice = gram_times(gathered.reshape(4 * rows, cols))

    step = coef_linear * iterate.astype(jnp.float32) + coef_cubic * once + coef_quintic * twice
    return (0.2 * math.sqrt(max(D, FF)) * step).astype(jnp.bfloat16)


def solution(mesh):
    axes = ("z_lo", "y", "z_hi", "x", "core")
    fine = Mesh(mesh.devices.reshape(4, 4, 4, 4, 2), axes)
    placed = P(axes[:2], axes[2:])
    return jax.shard_map(
        shards, mesh=fine, in_specs=(placed,), out_specs=placed, check_vma=False
    )
```

```python
import math

import jax
import jax.numpy as jnp
from jax import lax
from jax.experimental import pallas as pl
from jax.experimental.pallas import tpu as pltpu
from jax.sharding import Mesh
from jax.sharding import PartitionSpec as P

D = 3584
FF = 18432

coef_linear = 3.4445
coef_cubic = -4.775
coef_quintic = 2.0315

VMEM = pl.BlockSpec(memory_space=pltpu.VMEM)
SMEM = pl.BlockSpec(memory_space=pltpu.SMEM)


def call(kernel, shape, flops, *operands):
    return pl.pallas_call(
        kernel,
        out_shape=jax.ShapeDtypeStruct(shape, jnp.bfloat16),
        in_specs=[SMEM if operand.ndim == 1 else VMEM for operand in operands],
        out_specs=VMEM,
        compiler_params=pltpu.CompilerParams(vmem_limit_bytes=32 * 1024 * 1024),
        cost_estimate=pl.CostEstimate(
            flops=flops, bytes_accessed=8 * math.prod(shape), transcendentals=0
        ),
    )(*operands)


def dot(lhs, rhs, rhs_dim):
    return lax.dot_general(
        lhs, rhs, (((1,), (rhs_dim,)), ((), ())), preferred_element_type=jnp.float32
    )


def gram_kernel(core, left, right, out):
    blocks, cores, rows, cols = left.shape
    half = rows // 2
    start = pl.multiple_of(core[0] * half, 16)
    tile = jnp.zeros((blocks * half, blocks * rows), jnp.float32)
    for k in range(cores):
        lhs = left[:, k, pl.ds(start, half)].reshape(blocks * half, cols)
        tile += dot(lhs, right[:, k].reshape(blocks * rows, cols), 1)
    out[...] = tile.astype(out.dtype).reshape(out.shape)


def product_kernel(core, left, right, out):
    rhs = right[:, pl.ds(core[0], 1)].reshape(left.shape[1], out.shape[1])
    out[...] = dot(left[...], rhs, 0).astype(out.dtype)


def total(parts):
    return jnp.sum(parts.astype(jnp.float32), axis=0)


def gather(array, axes):
    return lax.all_gather(array.astype(jnp.float16), axes, axis=0).astype(jnp.bfloat16)


def shards(iterate):
    core = lax.axis_index("core").astype(jnp.int32).reshape(1)
    rows, cols = iterate.shape
    right = gather(iterate, ("z_lo", "core")).reshape(4, 2, rows, cols)
    left = gather(iterate, ("y", "core")).reshape(4, 2, rows, cols)

    tile = (4, rows // 2, 4 * rows)
    tile = call(gram_kernel, tile, 4 * math.prod(tile) * cols, core, left, right)
    piece = total(lax.all_to_all(tile, "x", 0, 0, tiled=True)).astype(jnp.bfloat16)
    piece = total(lax.all_gather(piece, "z_hi", axis=0)).astype(jnp.bfloat16)
    gram = gather(piece, ("x", "core")).reshape(4 * rows, 4 * rows)

    def gram_times(place, array):
        flops = 2 * gram.size * cols
        parts = call(product_kernel, (4 * rows, cols), flops, place, gram, array)
        return total(lax.all_to_all(parts.reshape(4, rows, cols), "y", 0, 0, tiled=True))

    once = gram_times(core, right)
    gathered = lax.all_gather(once.astype(jnp.bfloat16), "z_lo", axis=0)
    twice = gram_times(jnp.zeros_like(core), gathered.reshape(4, 1, rows, cols))

    step = coef_linear * iterate.astype(jnp.float32) + coef_cubic * once + coef_quintic * twice
    return (0.2 * math.sqrt(max(D, FF)) * step).astype(jnp.bfloat16)


def solution(mesh):
    axes = ("z_lo", "y", "z_hi", "x", "core")
    fine = Mesh(mesh.devices.reshape(4, 4, 4, 4, 2), axes)
    placed = P(axes[:2], axes[2:])
    return jax.shard_map(
        shards, mesh=fine, in_specs=(placed,), out_specs=placed, check_vma=False
    )
```

```python
import math

import jax
import jax.numpy as jnp
from jax import lax
from jax.experimental import pallas as pl
from jax.experimental.pallas import tpu as pltpu
from jax.sharding import Mesh
from jax.sharding import PartitionSpec as P

D = 3584
FF = 18432

coef_linear = 3.4445
coef_cubic = -4.775
coef_quintic = 2.0315

VMEM = pl.BlockSpec(memory_space=pltpu.VMEM)


def call(kernel, shape, flops, *operands):
    return pl.pallas_call(
        kernel,
        out_shape=jax.ShapeDtypeStruct(shape, jnp.bfloat16),
        in_specs=[VMEM] * len(operands),
        out_specs=VMEM,
        compiler_params=pltpu.CompilerParams(vmem_limit_bytes=32 * 1024 * 1024),
        cost_estimate=pl.CostEstimate(
            flops=flops, bytes_accessed=8 * math.prod(shape), transcendentals=0
        ),
    )(*operands)


def dot(lhs, rhs, rhs_dim):
    return lax.dot_general(
        lhs, rhs, (((1,), (rhs_dim,)), ((), ())), preferred_element_type=jnp.float32
    )


def copies_kernel(array, out, sems):
    copies = [
        pltpu.make_async_copy(array, out.at[i], sems.at[i]) for i in range(out.shape[0])
    ]
    for copy in copies:
        copy.start()
    for copy in copies:
        copy.wait()


def copies(array, count):
    return pl.pallas_call(
        copies_kernel,
        out_shape=jax.ShapeDtypeStruct((count,) + array.shape, array.dtype),
        in_specs=[pl.BlockSpec(memory_space=pl.ANY)],
        out_specs=pl.BlockSpec(memory_space=pltpu.HBM),
        scratch_shapes=[pltpu.SemaphoreType.DMA((count,))],
    )(array)


def gram_kernel(left, right, out):
    blocks, cores, rows, cols = left.shape
    tile = jnp.zeros((blocks * rows, out.shape[-1]), jnp.float32)
    for k in range(cores):
        lhs = left[:, k].reshape(blocks * rows, cols)
        tile += dot(lhs, right[:, k].reshape(out.shape[-1], cols), 1)
    out[...] = tile.astype(out.dtype).reshape(out.shape)


def product_kernel(left, right, out):
    out[...] = dot(left[...], right[...], 0).astype(out.dtype)


def total(parts):
    return jnp.sum(parts.astype(jnp.float32), axis=0)


def gather(array, axes):
    return lax.all_gather(array.astype(jnp.float16), axes, axis=0)


def shards(iterate):
    rows, cols = iterate.shape
    left = copies(iterate.reshape(2, rows // 2, cols), 4).reshape(8, rows // 2, cols)
    left = lax.all_to_all(left, ("y", "core"), 0, 0, tiled=True)
    left = left.reshape(4, 2, rows // 2, cols)
    right = gather(iterate, ("z_lo", "core")).reshape(4, 2, rows, cols)
    own = lax.dynamic_index_in_dim(right, lax.axis_index("core"), 1, keepdims=False)
    own = own.astype(jnp.bfloat16).reshape(4 * rows, cols)

    tile = (4, rows // 2, 4 * rows)
    flops = 4 * math.prod(tile) * cols
    tile = call(gram_kernel, tile, flops, left, right.astype(jnp.bfloat16))
    piece = total(lax.all_to_all(tile, "x", 0, 0, tiled=True)).astype(jnp.bfloat16)
    piece = total(lax.all_gather(piece, "z_hi", axis=0)).astype(jnp.bfloat16)
    gram = gather(piece, ("x", "core")).astype(jnp.bfloat16).reshape(4 * rows, 4 * rows)

    def gram_times(array):
        flops = 2 * gram.size * cols
        parts = call(product_kernel, array.shape, flops, gram, array)
        return total(lax.all_to_all(parts.reshape(4, rows, cols), "y", 0, 0, tiled=True))

    once = gram_times(own)
    gathered = lax.all_gather(once.astype(jnp.bfloat16), "z_lo", axis=0)
    twice = gram_times(gathered.reshape(4 * rows, cols))

    step = coef_linear * iterate.astype(jnp.float32) + coef_cubic * once + coef_quintic * twice
    return (0.2 * math.sqrt(max(D, FF)) * step).astype(jnp.bfloat16)


def solution(mesh):
    axes = ("z_lo", "y", "z_hi", "x", "core")
    fine = Mesh(mesh.devices.reshape(4, 4, 4, 4, 2), axes)
    placed = P(axes[:2], axes[2:])
    return jax.shard_map(
        shards, mesh=fine, in_specs=(placed,), out_specs=placed, check_vma=False
    )
```

```python
import math

import jax
import jax.numpy as jnp
from jax import lax
from jax.experimental import pallas as pl
from jax.experimental.pallas import tpu as pltpu
from jax.sharding import Mesh
from jax.sharding import PartitionSpec as P

D = 3584
FF = 18432

coef_linear = 3.4445
coef_cubic = -4.775
coef_quintic = 2.0315

VMEM = pl.BlockSpec(memory_space=pltpu.VMEM)
SMEM = pl.BlockSpec(memory_space=pltpu.SMEM)


def call(kernel, shapes, flops, *operands):
    shapes = [jax.ShapeDtypeStruct(shape, jnp.bfloat16) for shape in shapes]
    size = sum(2 * math.prod(array.shape) for array in (*shapes, *operands))
    return pl.pallas_call(
        kernel,
        out_shape=shapes,
        in_specs=[SMEM if operand.ndim == 1 else VMEM for operand in operands],
        out_specs=[VMEM] * len(shapes),
        compiler_params=pltpu.CompilerParams(vmem_limit_bytes=24 * 1024 * 1024),
        cost_estimate=pl.CostEstimate(flops=flops, bytes_accessed=size, transcendentals=0),
    )(*operands)


def dot(lhs, rhs, rhs_dim):
    return lax.dot_general(
        lhs, rhs, (((1,), (rhs_dim,)), ((), ())), preferred_element_type=jnp.float32
    )


def copies_kernel(array, out, held, sems):
    count = out.shape[0]
    fetch = pltpu.make_async_copy(array, held, sems.at[count])
    fetch.start()
    fetch.wait()
    copies = [pltpu.make_async_copy(held, out.at[i], sems.at[i]) for i in range(count)]
    for copy in copies:
        copy.start()
    for copy in copies:
        copy.wait()


def copies(array, count):
    return pl.pallas_call(
        copies_kernel,
        out_shape=jax.ShapeDtypeStruct((count,) + array.shape, array.dtype),
        in_specs=[pl.BlockSpec(memory_space=pl.ANY)],
        out_specs=pl.BlockSpec(memory_space=pltpu.HBM),
        scratch_shapes=[
            pltpu.VMEM(array.shape, array.dtype),
            pltpu.SemaphoreType.DMA((count + 1,)),
        ],
        compiler_params=pltpu.CompilerParams(vmem_limit_bytes=8 * 1024 * 1024),
    )(array)


def gram_kernel(core, left, right, out, own):
    blocks, cores, rows, cols = left.shape
    tile = jnp.zeros((blocks * rows, out.shape[-1]), jnp.float32)
    for k in range(cores):
        lhs = left[:, k].reshape(blocks * rows, cols)
        tile += dot(lhs, right[:, k].reshape(out.shape[-1], cols), 1)
    out[...] = tile.astype(out.dtype).reshape(out.shape)
    own[...] = right[:, pl.ds(core[0], 1)].reshape(own.shape)


def product_kernel(left, right, out):
    out[...] = dot(left[...], right[...], 0).astype(out.dtype)


def total(parts):
    return jnp.sum(parts.astype(jnp.float32), axis=0)


def gather(array, axes):
    return lax.all_gather(array.astype(jnp.float16), axes, axis=0)


def shards(iterate):
    rows, cols = iterate.shape
    left = copies(iterate.reshape(2, rows // 2, cols), 4).reshape(8, rows // 2, cols)
    left = lax.all_to_all(left, ("y", "core"), 0, 0, tiled=True)
    left = left.reshape(4, 2, rows // 2, cols)
    right = gather(iterate, ("z_lo", "core")).reshape(4, 2, rows, cols)

    shapes = (4, rows // 2, 4 * rows), (4 * rows, cols)
    flops = 4 * math.prod(shapes[0]) * cols
    core = lax.axis_index("core").astype(jnp.int32).reshape(1)
    tile, own = call(gram_kernel, shapes, flops, core, left, right.astype(jnp.bfloat16))
    piece = total(lax.all_to_all(tile, "x", 0, 0, tiled=True)).astype(jnp.bfloat16)
    piece = total(lax.all_gather(piece, "z_hi", axis=0)).astype(jnp.bfloat16)
    gram = gather(piece, ("x", "core")).astype(jnp.bfloat16).reshape(4 * rows, 4 * rows)

    def gram_times(array):
        flops = 2 * gram.size * cols
        (parts,) = call(product_kernel, [array.shape], flops, gram, array)
        return total(lax.all_to_all(parts.reshape(4, rows, cols), "y", 0, 0, tiled=True))

    once = gram_times(own)
    gathered = lax.all_gather(once.astype(jnp.bfloat16), "z_lo", axis=0)
    twice = gram_times(gathered.reshape(4 * rows, cols))

    step = coef_linear * iterate.astype(jnp.float32) + coef_cubic * once + coef_quintic * twice
    return (0.2 * math.sqrt(max(D, FF)) * step).astype(jnp.bfloat16)


def solution(mesh):
    axes = ("z_lo", "y", "z_hi", "x", "core")
    fine = Mesh(mesh.devices.reshape(4, 4, 4, 4, 2), axes)
    placed = P(axes[:2], axes[2:])
    return jax.shard_map(
        shards, mesh=fine, in_specs=(placed,), out_specs=placed, check_vma=False
    )
```

```python
import math

import jax
import jax.numpy as jnp
from jax import lax
from jax.experimental import pallas as pl
from jax.experimental.pallas import tpu as pltpu
from jax.sharding import Mesh
from jax.sharding import PartitionSpec as P

D = 3584
FF = 18432

coef_linear = 3.4445
coef_cubic = -4.775
coef_quintic = 2.0315

VMEM = pl.BlockSpec(memory_space=pltpu.VMEM)
SMEM = pl.BlockSpec(memory_space=pltpu.SMEM)
HBM = pl.BlockSpec(memory_space=pltpu.HBM)
ANY = pl.BlockSpec(memory_space=pl.ANY)

SAME_Y = [[4 * y + (s - y) % 4 for s in range(4)] for y in range(4)]
SAME_X = [[4 * ((s - x) % 4) + x for s in range(4)] for x in range(4)]
SAME_S = [[4 * y + (s - y) % 4 for y in range(4)] for s in range(4)]


def with_cores(groups):
    return [[2 * chip + core for chip in group for core in range(2)] for group in groups]


def call(kernel, operands, outputs, scratch=(), flops=0):
    arrays, in_specs = zip(*operands)
    shapes, out_specs = zip(*outputs)
    shapes = [jax.ShapeDtypeStruct(shape, jnp.bfloat16) for shape in shapes]
    size = sum(2 * math.prod(array.shape) for array in (*shapes, *arrays))
    return pl.pallas_call(
        kernel,
        out_shape=shapes,
        in_specs=in_specs,
        out_specs=out_specs,
        scratch_shapes=scratch,
        compiler_params=pltpu.CompilerParams(vmem_limit_bytes=24 * 1024 * 1024),
        cost_estimate=pl.CostEstimate(flops=flops, bytes_accessed=size, transcendentals=0),
    )(*arrays)


def dot(lhs, rhs, contract=(1, 0)):
    return lax.dot_general(
        lhs, rhs, ((contract[:1], contract[1:]), ((), ())), preferred_element_type=jnp.float32
    )


def start_copies(source, out, sems):
    copies = [pltpu.make_async_copy(source, out.at[i], sems.at[i]) for i in range(out.shape[0])]
    for copy in copies:
        copy.start()
    return copies


def wait(copies):
    for copy in copies:
        copy.wait()


def copies_kernel(array, out, sems):
    wait(start_copies(array, out, sems))


def gram_kernel(core, left, right, tile, spread, sems):
    copies = start_copies(right.at[:, core[0]], spread, sems)
    blocks, cores, rows, cols = left.shape
    sums = jnp.zeros((blocks * rows, tile.shape[-1]), jnp.float32)
    for k in range(cores):
        lhs = left[:, k].reshape(blocks * rows, cols)
        sums += dot(lhs, right[:, k].reshape(tile.shape[-1], cols), (1, 1))
    tile[...] = sums.astype(tile.dtype).reshape(tile.shape)
    wait(copies)


def piece_kernel(parts, piece, spread, sems):
    piece[...] = jnp.sum(parts[...].astype(jnp.float32), axis=0).astype(piece.dtype)
    wait(start_copies(piece, spread, sems))


def first_kernel(band, whole, out, held, sems):
    blocks, cores, rows, inner = band.shape
    copies = [pltpu.make_async_copy(whole.at[y], held.at[y], sems.at[y]) for y in range(blocks)]
    for copy in copies:
        copy.start()
    sums = jnp.zeros((cores * rows, out.shape[-1]), jnp.float32)
    for y in range(blocks):
        copies[y].wait()
        sums += dot(band[y].reshape(cores * rows, inner), held[y])
    out[...] = sums.astype(out.dtype)


def second_kernel(tile, once, out):
    out[...] = dot(tile[...], once[...], (0, 0)).astype(out.dtype)


def total(parts):
    return jnp.sum(parts.astype(jnp.float32), axis=0)


def gather(array, axes, groups=None):
    array = array.astype(jnp.float16)
    array = lax.all_gather(array, axes, axis=0, axis_index_groups=groups)
    return array.astype(jnp.bfloat16)


def exchange(array, axes, groups=None):
    return lax.all_to_all(array, axes, 0, 0, tiled=True, axis_index_groups=groups)


def shards(iterate):
    rows, cols = iterate.shape
    half, plane = rows // 2, ("y", "x", "core")
    core = lax.axis_index("core").astype(jnp.int32).reshape(1)
    sems = pltpu.SemaphoreType.DMA

    halves = iterate.reshape(2, half, cols)
    (left,) = call(
        copies_kernel, [(halves, VMEM)], [((4, 2, half, cols), HBM)], [sems((4,))]
    )
    left = exchange(left.reshape(8, half, cols), ("y", "core")).reshape(4, 2, half, cols)
    right = gather(iterate, ("z_lo", "core")).reshape(4, 2, rows, cols)

    tile, spread = call(
        gram_kernel,
        [(core, SMEM), (left, VMEM), (right, VMEM)],
        [((4, half, 4 * rows), VMEM), ((4, 4, rows, cols), HBM)],
        [sems((4,))],
        flops=4 * 4 * half * 4 * rows * cols,
    )
    whole = exchange(spread, "y").reshape(4, 4 * rows, cols)
    piece = total(exchange(tile, ("y", "x"), SAME_Y)).astype(jnp.bfloat16)
    piece, spread = call(
        piece_kernel,
        [(lax.all_gather(piece, "z_hi", axis=0), VMEM)],
        [((half, 4 * rows), VMEM), ((8, half, 4 * rows), HBM)],
        [sems((8,))],
    )

    tile = exchange(spread, plane, with_cores(SAME_Y)).reshape(4 * rows, 4 * rows)
    band = gather(piece, plane, with_cores(SAME_S)).reshape(4, 2, half, 4 * rows)
    (once,) = call(
        first_kernel,
        [(band, VMEM), (whole, ANY)],
        [((rows, cols), VMEM)],
        [pltpu.VMEM(whole.shape, whole.dtype), sems((4,))],
        flops=2 * rows * 16 * rows * cols,
    )
    once = lax.all_gather(once, ("y", "x"), axis=0, axis_index_groups=SAME_X)
    (parts,) = call(
        second_kernel,
        [(tile, VMEM), (once.reshape(4 * rows, cols), VMEM)],
        [((4 * rows, cols), VMEM)],
        flops=2 * tile.size * cols,
    )
    twice = total(exchange(parts.reshape(4, rows, cols), "z_lo"))
    once = lax.dynamic_index_in_dim(once, lax.axis_index("y"), 0, keepdims=False)

    step = coef_linear * iterate.astype(jnp.float32) + coef_cubic * once.astype(jnp.float32)
    step = step + coef_quintic * twice
    return (0.2 * math.sqrt(max(D, FF)) * step).astype(jnp.bfloat16)


def solution(mesh):
    axes = ("z_lo", "y", "z_hi", "x", "core")
    fine = Mesh(mesh.devices.reshape(4, 4, 4, 4, 2), axes)
    placed = P(axes[:2], axes[2:])
    return jax.shard_map(
        shards, mesh=fine, in_specs=(placed,), out_specs=placed, check_vma=False
    )
```

```python
import math

import jax
import jax.numpy as jnp
from jax import lax
from jax.experimental import pallas as pl
from jax.experimental.pallas import tpu as pltpu
from jax.sharding import Mesh
from jax.sharding import PartitionSpec as P

D = 3584
FF = 18432

coef_linear = 3.4445
coef_cubic = -4.775
coef_quintic = 2.0315

SWAP = [(0, 1), (1, 0)]
VMEM = pl.BlockSpec(memory_space=pltpu.VMEM)
SMEM = pl.BlockSpec(memory_space=pltpu.SMEM)
HBM = pl.BlockSpec(memory_space=pltpu.HBM)
ANY = pl.BlockSpec(memory_space=pl.ANY)


def call(kernel, operands, output, spec=VMEM, scratch=(), flops=0):
    arrays, in_specs = zip(*operands)
    return pl.pallas_call(
        kernel,
        out_shape=output,
        in_specs=in_specs,
        out_specs=spec,
        scratch_shapes=scratch,
        compiler_params=pltpu.CompilerParams(vmem_limit_bytes=24 * 1024 * 1024),
        cost_estimate=pl.CostEstimate(
            flops=flops,
            bytes_accessed=2 * sum(math.prod(array.shape) for array in (output, *arrays)),
            transcendentals=0,
        ),
    )(*arrays)


def bf16(*shape):
    return jax.ShapeDtypeStruct(shape, jnp.bfloat16)


def f32(*shape):
    return jax.ShapeDtypeStruct(shape, jnp.float32)


def dot(lhs, rhs, rhs_dim):
    return lax.dot_general(
        lhs, rhs, (((1,), (rhs_dim,)), ((), ())), preferred_element_type=jnp.float32
    )


def copies_kernel(array, out, held, sems):
    count = out.shape[0]
    fetch = pltpu.make_async_copy(array, held, sems.at[count])
    fetch.start()
    fetch.wait()
    copies = [pltpu.make_async_copy(held, out.at[i], sems.at[i]) for i in range(count)]
    for copy in copies:
        copy.start()
    for copy in copies:
        copy.wait()


def gram_kernel(which, left, right, out):
    blocks, rows, cols = left.shape
    half = rows // 2
    start = pl.multiple_of(which[0] * half, 16)
    lhs = left[:, pl.ds(start, half)].reshape(blocks * half, cols)
    tile = dot(lhs, right[...].reshape(out.shape[-1], cols), 1)
    out[...] = tile.astype(out.dtype).reshape(out.shape)


def product_kernel(left, right, out, held, sems):
    blocks, rows, cols = right.shape
    copies = [pltpu.make_async_copy(right.at[i], held.at[i], sems.at[i]) for i in range(blocks)]
    for copy in copies:
        copy.start()
    sums = jnp.zeros(out.shape, jnp.float32)
    for i in range(blocks):
        copies[i].wait()
        sums += dot(left[:, i * rows : (i + 1) * rows], held[i], 0)
    out[...] = sums.astype(out.dtype)


def update_kernel(iterate, once, parts, out, held, sem):
    fetch = pltpu.make_async_copy(iterate, held, sem)
    fetch.start()
    step = coef_cubic * once[...]
    step += coef_quintic * jnp.sum(parts[...].astype(jnp.float32), axis=0)
    fetch.wait()
    step += coef_linear * held[...].astype(jnp.float32)
    out[...] = (0.2 * math.sqrt(max(D, FF)) * step).astype(out.dtype)


def total(parts):
    return jnp.sum(parts.astype(jnp.float32), axis=0)


def exchange(array, axes):
    return lax.all_to_all(array, axes, 0, 0, tiled=True)


def shards(iterate):
    rows, cols = iterate.shape
    half = rows // 2
    core = lax.axis_index("core").astype(jnp.int32).reshape(1)
    sems = pltpu.SemaphoreType.DMA

    left = call(
        copies_kernel,
        [(iterate, ANY)],
        bf16(4, rows, cols),
        spec=HBM,
        scratch=[pltpu.VMEM(iterate.shape, iterate.dtype), sems((5,))],
    )
    left = exchange(left, "y")
    right = lax.all_gather(iterate, "z_lo", axis=0)

    def half_tile(which, output):
        operands = [(which, SMEM), (left, VMEM), (right, VMEM)]
        return call(gram_kernel, operands, output, flops=2 * 4 * half * 4 * rows * cols)

    shape = (4, half, 4 * rows)
    away = lax.ppermute(half_tile(1 - core, bf16(*shape)), "core", SWAP)
    tile = (half_tile(core, f32(*shape)) + away.astype(jnp.float32)).astype(jnp.bfloat16)
    piece = total(exchange(tile, "x")).astype(jnp.bfloat16)
    piece = total(lax.all_gather(piece, "z_hi", axis=0)).astype(jnp.bfloat16)
    gram = lax.all_gather(piece.astype(jnp.float16), ("x", "core"), axis=0)
    gram = gram.astype(jnp.bfloat16).reshape(4 * rows, 4 * rows)

    def gram_times(array):
        parts = call(
            product_kernel,
            [(gram, VMEM), (array, ANY)],
            bf16(4 * rows, cols),
            scratch=[pltpu.VMEM(array.shape, array.dtype), sems((4,))],
            flops=2 * gram.size * cols,
        )
        return exchange(parts.reshape(4, rows, cols), "y")

    once = total(gram_times(right))
    twice = gram_times(lax.all_gather(once.astype(jnp.bfloat16), "z_lo", axis=0))
    return call(
        update_kernel,
        [(iterate, ANY), (once, VMEM), (twice, VMEM)],
        bf16(rows, cols),
        scratch=[pltpu.VMEM(iterate.shape, iterate.dtype), sems],
    )


def solution(mesh):
    axes = ("z_lo", "y", "z_hi", "x", "core")
    fine = Mesh(mesh.devices.reshape(4, 4, 4, 4, 2), axes)
    placed = P(axes[:2], axes[2:])
    return jax.shard_map(
        shards, mesh=fine, in_specs=(placed,), out_specs=placed, check_vma=False
    )
```

```python
import math

import jax
import jax.numpy as jnp
from jax import lax
from jax.experimental import pallas as pl
from jax.experimental.pallas import tpu as pltpu
from jax.sharding import Mesh
from jax.sharding import PartitionSpec as P

D = 3584
FF = 18432

coef_linear = 3.4445
coef_cubic = -4.775
coef_quintic = 2.0315

VMEM = pl.BlockSpec(memory_space=pltpu.VMEM)
SMEM = pl.BlockSpec(memory_space=pltpu.SMEM)
HBM = pl.BlockSpec(memory_space=pltpu.HBM)
ANY = pl.BlockSpec(memory_space=pl.ANY)


def call(kernel, operands, output, spec=VMEM, scratch=(), flops=0):
    arrays, in_specs = zip(*operands)
    return pl.pallas_call(
        kernel,
        out_shape=output,
        in_specs=in_specs,
        out_specs=spec,
        scratch_shapes=scratch,
        compiler_params=pltpu.CompilerParams(vmem_limit_bytes=24 * 1024 * 1024),
        cost_estimate=pl.CostEstimate(
            flops=flops,
            bytes_accessed=2 * sum(math.prod(array.shape) for array in (output, *arrays)),
            transcendentals=0,
        ),
    )(*arrays)


def bf16(*shape):
    return jax.ShapeDtypeStruct(shape, jnp.bfloat16)


def dot(lhs, rhs, rhs_dim):
    return lax.dot_general(
        lhs, rhs, (((1,), (rhs_dim,)), ((), ())), preferred_element_type=jnp.float32
    )


def copies_kernel(array, out, sems):
    copies = [pltpu.make_async_copy(array, out.at[i], sems.at[i]) for i in range(out.shape[0])]
    for copy in copies:
        copy.start()
    for copy in copies:
        copy.wait()


def gram_kernel(left, right, out):
    blocks, cores, rows, cols = left.shape
    tile = jnp.zeros((blocks * rows, out.shape[-1]), jnp.float32)
    for k in range(cores):
        lhs = left[:, k].reshape(blocks * rows, cols)
        tile += dot(lhs, right[:, k].reshape(out.shape[-1], cols), 1)
    out[...] = tile.astype(out.dtype).reshape(out.shape)


def own_kernel(core, right, out):
    out[...] = right[:, pl.ds(core[0], 1)].reshape(out.shape)


def product_kernel(left, right, out):
    out[...] = dot(left[...], right[...], 0).astype(out.dtype)


def update_kernel(iterate, once, parts, out, held, sem):
    fetch = pltpu.make_async_copy(iterate, held, sem)
    fetch.start()
    step = coef_cubic * once[...]
    step += coef_quintic * jnp.sum(parts[...].astype(jnp.float32), axis=0)
    fetch.wait()
    step += coef_linear * held[...].astype(jnp.float32)
    out[...] = (0.2 * math.sqrt(max(D, FF)) * step).astype(out.dtype)


def total(parts):
    return jnp.sum(parts.astype(jnp.float32), axis=0)


def gather(array, axes):
    return lax.all_gather(array.astype(jnp.float16), axes, axis=0).astype(jnp.bfloat16)


def exchange(array, axes):
    return lax.all_to_all(array, axes, 0, 0, tiled=True)


def shards(iterate):
    rows, cols = iterate.shape
    half = rows // 2
    core = lax.axis_index("core").astype(jnp.int32).reshape(1)
    sems = pltpu.SemaphoreType.DMA

    left = call(
        copies_kernel,
        [(iterate.reshape(2, half, cols), VMEM)],
        bf16(4, 2, half, cols),
        spec=HBM,
        scratch=[sems((4,))],
    )
    left = exchange(left.reshape(8, half, cols), ("y", "core")).reshape(4, 2, half, cols)
    right = gather(iterate, ("z_lo", "core")).reshape(4, 2, rows, cols)
    own = call(own_kernel, [(core, SMEM), (right, VMEM)], bf16(4 * rows, cols))

    tile = call(
        gram_kernel,
        [(left, VMEM), (right, VMEM)],
        bf16(4, half, 4 * rows),
        flops=4 * 4 * half * 4 * rows * cols,
    )
    piece = total(exchange(tile, "x")).astype(jnp.bfloat16)
    piece = total(lax.all_gather(piece, "z_hi", axis=0)).astype(jnp.bfloat16)
    gram = gather(piece, ("x", "core")).reshape(4 * rows, 4 * rows)

    def gram_times(array):
        parts = call(
            product_kernel,
            [(gram, VMEM), (array, VMEM)],
            bf16(4 * rows, cols),
            flops=2 * gram.size * cols,
        )
        return exchange(parts.reshape(4, rows, cols), "y")

    once = total(gram_times(own))
    gathered = lax.all_gather(once.astype(jnp.bfloat16), "z_lo", axis=0)
    twice = gram_times(gathered.reshape(4 * rows, cols))
    return call(
        update_kernel,
        [(iterate, ANY), (once, VMEM), (twice, VMEM)],
        bf16(rows, cols),
        scratch=[pltpu.VMEM(iterate.shape, iterate.dtype), sems],
    )


def solution(mesh):
    axes = ("z_lo", "y", "z_hi", "x", "core")
    fine = Mesh(mesh.devices.reshape(4, 4, 4, 4, 2), axes)
    placed = P(axes[:2], axes[2:])
    return jax.shard_map(
        shards, mesh=fine, in_specs=(placed,), out_specs=placed, check_vma=False
    )
```

```python
import math

import jax
import jax.numpy as jnp
from jax import lax
from jax.experimental import pallas as pl
from jax.experimental.pallas import tpu as pltpu
from jax.sharding import Mesh
from jax.sharding import PartitionSpec as P

D = 3584
FF = 18432

coef_linear = 3.4445
coef_cubic = -4.775
coef_quintic = 2.0315

LANES = 128
VMEM = pl.BlockSpec(memory_space=pltpu.VMEM)
SMEM = pl.BlockSpec(memory_space=pltpu.SMEM)
HBM = pl.BlockSpec(memory_space=pltpu.HBM)
ANY = pl.BlockSpec(memory_space=pl.ANY)


def call(kernel, operands, output, spec=VMEM, scratch=(), flops=0):
    arrays, in_specs = zip(*operands)
    return pl.pallas_call(
        kernel,
        out_shape=output,
        in_specs=in_specs,
        out_specs=spec,
        scratch_shapes=scratch,
        compiler_params=pltpu.CompilerParams(vmem_limit_bytes=24 * 1024 * 1024),
        cost_estimate=pl.CostEstimate(
            flops=flops,
            bytes_accessed=2 * sum(math.prod(array.shape) for array in (output, *arrays)),
            transcendentals=0,
        ),
    )(*arrays)


def bf16(*shape):
    return jax.ShapeDtypeStruct(shape, jnp.bfloat16)


def dot(lhs, rhs, rhs_dim):
    return lax.dot_general(
        lhs, rhs, (((1,), (rhs_dim,)), ((), ())), preferred_element_type=jnp.float32
    )


def copies_kernel(array, out, sems):
    copies = [pltpu.make_async_copy(array, out.at[i], sems.at[i]) for i in range(out.shape[0])]
    for copy in copies:
        copy.start()
    for copy in copies:
        copy.wait()


def gram_kernel(left, right, out):
    blocks, cores, rows, cols = left.shape
    tile = jnp.zeros((blocks * rows, out.shape[-1]), jnp.float32)
    for k in range(cores):
        lhs = left[:, k].reshape(blocks * rows, cols)
        tile += dot(lhs, right[:, k].reshape(out.shape[-1], cols), 1)
    out[...] = tile.astype(out.dtype).reshape(out.shape)


def own_kernel(core, right, out):
    out[...] = right[:, pl.ds(core[0], 1)].reshape(out.shape)


def pieces(rows, cols):
    whole, rest = cols // LANES, cols % LANES
    for k in range(whole):
        yield slice(0, rows), slice(k * LANES, (k + 1) * LANES), slice(k * rows, (k + 1) * rows), slice(0, LANES)
    each = rows * rest // LANES
    for k in range(LANES // rest if rest else 0):
        columns = slice(k * rest, (k + 1) * rest)
        yield slice(k * each, (k + 1) * each), slice(whole * LANES, cols), slice(whole * rows, whole * rows + each), columns


def first_kernel(left, right, out):
    product = dot(left[...], right[...], 0).astype(out.dtype)
    rows = product.shape[0] // out.shape[0]
    for i in range(out.shape[0]):
        block = product[i * rows : (i + 1) * rows]
        for row, col, packed_row, packed_col in pieces(rows, product.shape[1]):
            out[i, packed_row, packed_col] = block[row, col]


def second_kernel(left, right, out, held):
    rows = held.shape[0] // right.shape[0]
    for i in range(right.shape[0]):
        for row, col, packed_row, packed_col in pieces(rows, held.shape[1]):
            row = slice(i * rows + row.start, i * rows + row.stop)
            held[row, col] = right[i, packed_row, packed_col]
    first_kernel(left, held, out)


def update_kernel(iterate, once, parts, out, held, sem):
    fetch = pltpu.make_async_copy(iterate, held, sem)
    fetch.start()
    packed = coef_cubic * once[...]
    packed += coef_quintic * jnp.sum(parts[...].astype(jnp.float32), axis=0)
    fetch.wait()
    for row, col, packed_row, packed_col in pieces(*out.shape):
        step = coef_linear * held[row, col].astype(jnp.float32) + packed[packed_row, packed_col]
        out[row, col] = (0.2 * math.sqrt(max(D, FF)) * step).astype(out.dtype)


def total(parts):
    return jnp.sum(parts.astype(jnp.float32), axis=0)


def gather(array, axes):
    return lax.all_gather(array.astype(jnp.float16), axes, axis=0).astype(jnp.bfloat16)


def exchange(array, axes):
    return lax.all_to_all(array, axes, 0, 0, tiled=True)


def shards(iterate):
    rows, cols = iterate.shape
    half = rows // 2
    core = lax.axis_index("core").astype(jnp.int32).reshape(1)
    sems = pltpu.SemaphoreType.DMA

    left = call(
        copies_kernel,
        [(iterate.reshape(2, half, cols), VMEM)],
        bf16(4, 2, half, cols),
        spec=HBM,
        scratch=[sems((4,))],
    )
    left = exchange(left.reshape(8, half, cols), ("y", "core")).reshape(4, 2, half, cols)
    right = gather(iterate, ("z_lo", "core")).reshape(4, 2, rows, cols)
    own = call(own_kernel, [(core, SMEM), (right, VMEM)], bf16(4 * rows, cols))
    right, own = lax.optimization_barrier((right, own))

    tile = call(
        gram_kernel,
        [(left, VMEM), (right, VMEM)],
        bf16(4, half, 4 * rows),
        flops=4 * 4 * half * 4 * rows * cols,
    )
    piece = total(exchange(tile, "x")).astype(jnp.bfloat16)
    piece = total(lax.all_gather(piece, "z_hi", axis=0)).astype(jnp.bfloat16)
    gram = gather(piece, ("x", "core")).reshape(4 * rows, 4 * rows)

    packed = bf16(4, rows * cols // LANES, LANES)
    flops = 2 * gram.size * cols
    once = call(first_kernel, [(gram, VMEM), (own, VMEM)], packed, flops=flops)
    once = total(exchange(once, "y"))
    twice = call(
        second_kernel,
        [(gram, VMEM), (lax.all_gather(once.astype(jnp.bfloat16), "z_lo", axis=0), VMEM)],
        packed,
        scratch=[pltpu.VMEM(own.shape, own.dtype)],
        flops=flops,
    )
    return call(
        update_kernel,
        [(iterate, ANY), (once, VMEM), (exchange(twice, "y"), VMEM)],
        bf16(rows, cols),
        scratch=[pltpu.VMEM(iterate.shape, iterate.dtype), sems],
    )


def solution(mesh):
    axes = ("z_lo", "y", "z_hi", "x", "core")
    fine = Mesh(mesh.devices.reshape(4, 4, 4, 4, 2), axes)
    placed = P(axes[:2], axes[2:])
    return jax.shard_map(
        shards, mesh=fine, in_specs=(placed,), out_specs=placed, check_vma=False
    )
```

```python
import math

import jax
import jax.numpy as jnp
from jax import lax
from jax.experimental import pallas as pl
from jax.experimental.pallas import tpu as pltpu
from jax.sharding import Mesh
from jax.sharding import PartitionSpec as P

D = 3584
FF = 18432

coef_linear = 3.4445
coef_cubic = -4.775
coef_quintic = 2.0315

LANES = 128
VMEM = pl.BlockSpec(memory_space=pltpu.VMEM)
SMEM = pl.BlockSpec(memory_space=pltpu.SMEM)
HBM = pl.BlockSpec(memory_space=pltpu.HBM)
ANY = pl.BlockSpec(memory_space=pl.ANY)


def call(kernel, operands, output, spec=VMEM, scratch=(), flops=0):
    arrays, in_specs = zip(*operands)
    return pl.pallas_call(
        kernel,
        out_shape=output,
        in_specs=in_specs,
        out_specs=spec,
        scratch_shapes=scratch,
        compiler_params=pltpu.CompilerParams(vmem_limit_bytes=16 * 1024 * 1024),
        cost_estimate=pl.CostEstimate(
            flops=flops,
            bytes_accessed=2 * sum(math.prod(array.shape) for array in (output, *arrays)),
            transcendentals=0,
        ),
    )(*arrays)


def bf16(*shape):
    return jax.ShapeDtypeStruct(shape, jnp.bfloat16)


def dot(lhs, rhs, rhs_dim):
    return lax.dot_general(
        lhs, rhs, (((1,), (rhs_dim,)), ((), ())), preferred_element_type=jnp.float32
    )


def copies_kernel(array, out, sems):
    copies = [pltpu.make_async_copy(array, out.at[i], sems.at[i]) for i in range(out.shape[0])]
    for copy in copies:
        copy.start()
    for copy in copies:
        copy.wait()


def gram_kernel(left, right, out):
    blocks, cores, rows, cols = left.shape
    tile = jnp.zeros((blocks * rows, out.shape[-1]), jnp.float32)
    for k in range(cores):
        lhs = left[:, k].reshape(blocks * rows, cols)
        tile += dot(lhs, right[:, k].reshape(out.shape[-1], cols), 1)
    out[...] = tile.astype(out.dtype).reshape(out.shape)


def own_kernel(core, right, out):
    out[...] = right[:, pl.ds(core[0], 1)].reshape(out.shape)


def pieces(rows, cols):
    whole, rest = cols // LANES, cols % LANES
    for k in range(whole):
        yield slice(0, rows), slice(k * LANES, (k + 1) * LANES), slice(k * rows, (k + 1) * rows), slice(0, LANES)
    each = rows * rest // LANES
    for k in range(LANES // rest if rest else 0):
        columns = slice(k * rest, (k + 1) * rest)
        yield slice(k * each, (k + 1) * each), slice(whole * LANES, cols), slice(whole * rows, whole * rows + each), columns


def first_kernel(left, right, out):
    product = dot(left[...], right[...], 0).astype(out.dtype)
    rows = product.shape[0] // out.shape[0]
    for i in range(out.shape[0]):
        block = product[i * rows : (i + 1) * rows]
        for row, col, packed_row, packed_col in pieces(rows, product.shape[1]):
            out[i, packed_row, packed_col] = block[row, col]


def second_kernel(left, right, out, held):
    rows = held.shape[0] // right.shape[0]
    for i in range(right.shape[0]):
        for row, col, packed_row, packed_col in pieces(rows, held.shape[1]):
            row = slice(i * rows + row.start, i * rows + row.stop)
            held[row, col] = right[i, packed_row, packed_col]
    first_kernel(left, held, out)


def update_kernel(iterate, once, parts, out, held, sem):
    fetch = pltpu.make_async_copy(iterate, held, sem)
    fetch.start()
    packed = coef_cubic * once[...]
    packed += coef_quintic * jnp.sum(parts[...].astype(jnp.float32), axis=0)
    fetch.wait()
    for row, col, packed_row, packed_col in pieces(*out.shape):
        step = coef_linear * held[row, col].astype(jnp.float32) + packed[packed_row, packed_col]
        out[row, col] = (0.2 * math.sqrt(max(D, FF)) * step).astype(out.dtype)


def total(parts):
    return jnp.sum(parts.astype(jnp.float32), axis=0)


def gather(array, axes):
    return lax.all_gather(array.astype(jnp.float16), axes, axis=0).astype(jnp.bfloat16)


def exchange(array, axes):
    return lax.all_to_all(array, axes, 0, 0, tiled=True)


def shards(iterate):
    rows, cols = iterate.shape
    half = rows // 2
    core = lax.axis_index("core").astype(jnp.int32).reshape(1)
    sems = pltpu.SemaphoreType.DMA

    left = call(
        copies_kernel,
        [(iterate.reshape(2, half, cols), VMEM)],
        bf16(4, 2, half, cols),
        spec=HBM,
        scratch=[sems((4,))],
    )
    left = exchange(left.reshape(8, half, cols), ("y", "core")).reshape(4, 2, half, cols)
    right = gather(iterate, ("z_lo", "core")).reshape(4, 2, rows, cols)

    tile = call(
        gram_kernel,
        [(left, VMEM), (right, VMEM)],
        bf16(4, half, 4 * rows),
        flops=4 * 4 * half * 4 * rows * cols,
    )
    tile, right = lax.optimization_barrier((tile, right))
    own = call(own_kernel, [(core, SMEM), (right, VMEM)], bf16(4 * rows, cols))
    tile, own = lax.optimization_barrier((tile, own))
    piece = total(exchange(tile, "x")).astype(jnp.bfloat16)
    piece = total(lax.all_gather(piece, "z_hi", axis=0)).astype(jnp.bfloat16)
    gram = gather(piece, ("x", "core")).reshape(4 * rows, 4 * rows)

    packed = bf16(4, rows * cols // LANES, LANES)
    flops = 2 * gram.size * cols
    once = call(first_kernel, [(gram, VMEM), (own, VMEM)], packed, flops=flops)
    once = total(exchange(once, "y"))
    twice = call(
        second_kernel,
        [(gram, VMEM), (lax.all_gather(once.astype(jnp.bfloat16), "z_lo", axis=0), VMEM)],
        packed,
        scratch=[pltpu.VMEM(own.shape, own.dtype)],
        flops=flops,
    )
    return call(
        update_kernel,
        [(iterate, ANY), (once, VMEM), (exchange(twice, "y"), VMEM)],
        bf16(rows, cols),
        scratch=[pltpu.VMEM(iterate.shape, iterate.dtype), sems],
    )


def solution(mesh):
    axes = ("z_lo", "y", "z_hi", "x", "core")
    fine = Mesh(mesh.devices.reshape(4, 4, 4, 4, 2), axes)
    placed = P(axes[:2], axes[2:])
    return jax.shard_map(
        shards, mesh=fine, in_specs=(placed,), out_specs=placed, check_vma=False
    )
```

```python
import math

import jax
import jax.numpy as jnp
from jax import lax
from jax.experimental import pallas as pl
from jax.experimental.pallas import tpu as pltpu
from jax.sharding import Mesh
from jax.sharding import PartitionSpec as P

D = 3584
FF = 18432

coef_linear = 3.4445
coef_cubic = -4.775
coef_quintic = 2.0315

LANES = 128
PAIRS = [[0, 2], [4, 6], [3, 5], [7, 1]], [[2, 4], [6, 0], [1, 3], [5, 7]]
VMEM = pl.BlockSpec(memory_space=pltpu.VMEM)
SMEM = pl.BlockSpec(memory_space=pltpu.SMEM)
HBM = pl.BlockSpec(memory_space=pltpu.HBM)
ANY = pl.BlockSpec(memory_space=pl.ANY)


def call(kernel, operands, output, spec=VMEM, scratch=(), flops=0):
    arrays, in_specs = zip(*operands)
    return pl.pallas_call(
        kernel,
        out_shape=output,
        in_specs=in_specs,
        out_specs=spec,
        scratch_shapes=scratch,
        compiler_params=pltpu.CompilerParams(vmem_limit_bytes=16 * 1024 * 1024),
        cost_estimate=pl.CostEstimate(
            flops=flops,
            bytes_accessed=2 * sum(math.prod(array.shape) for array in (output, *arrays)),
            transcendentals=0,
        ),
    )(*arrays)


def bf16(*shape):
    return jax.ShapeDtypeStruct(shape, jnp.bfloat16)


def dot(lhs, rhs, rhs_dim):
    return lax.dot_general(
        lhs, rhs, (((1,), (rhs_dim,)), ((), ())), preferred_element_type=jnp.float32
    )


def copies_kernel(array, out, sems):
    copies = [pltpu.make_async_copy(array, out.at[i], sems.at[i]) for i in range(out.shape[0])]
    for copy in copies:
        copy.start()
    for copy in copies:
        copy.wait()


def gram_kernel(left, right, out):
    blocks, cores, rows, cols = left.shape
    tile = jnp.zeros((blocks * rows, out.shape[-1]), jnp.float32)
    for k in range(cores):
        lhs = left[:, k].reshape(blocks * rows, cols)
        tile += dot(lhs, right[:, k].reshape(out.shape[-1], cols), 1)
    out[...] = tile.astype(out.dtype).reshape(out.shape)


def own_kernel(core, right, out):
    out[...] = right[:, pl.ds(core[0], 1)].reshape(out.shape)


def pieces(rows, cols):
    whole, rest = cols // LANES, cols % LANES
    for k in range(whole):
        yield slice(0, rows), slice(k * LANES, (k + 1) * LANES), slice(k * rows, (k + 1) * rows), slice(0, LANES)
    each = rows * rest // LANES
    for k in range(LANES // rest if rest else 0):
        columns = slice(k * rest, (k + 1) * rest)
        yield slice(k * each, (k + 1) * each), slice(whole * LANES, cols), slice(whole * rows, whole * rows + each), columns


def first_kernel(left, right, out):
    product = dot(left[...], right[...], 0).astype(out.dtype)
    rows = product.shape[0] // out.shape[0]
    for i in range(out.shape[0]):
        block = product[i * rows : (i + 1) * rows]
        for row, col, packed_row, packed_col in pieces(rows, product.shape[1]):
            out[i, packed_row, packed_col] = block[row, col]


def second_kernel(left, right, out, held):
    rows = held.shape[0] // right.shape[0]
    for i in range(right.shape[0]):
        for row, col, packed_row, packed_col in pieces(rows, held.shape[1]):
            row = slice(i * rows + row.start, i * rows + row.stop)
            held[row, col] = right[i, packed_row, packed_col]
    first_kernel(left, held, out)


def update_kernel(iterate, once, parts, out, held, sem):
    fetch = pltpu.make_async_copy(iterate, held, sem)
    fetch.start()
    packed = coef_cubic * once[...]
    packed += coef_quintic * jnp.sum(parts[...].astype(jnp.float32), axis=0)
    fetch.wait()
    for row, col, packed_row, packed_col in pieces(*out.shape):
        step = coef_linear * held[row, col].astype(jnp.float32) + packed[packed_row, packed_col]
        out[row, col] = (0.2 * math.sqrt(max(D, FF)) * step).astype(out.dtype)


def total(parts):
    return jnp.sum(parts.astype(jnp.float32), axis=0)


def gather(array, axes):
    return lax.all_gather(array.astype(jnp.float16), axes, axis=0).astype(jnp.bfloat16)


def exchange(array, axes):
    return lax.all_to_all(array, axes, 0, 0, tiled=True)


def shards(iterate):
    rows, cols = iterate.shape
    half = rows // 2
    core = lax.axis_index("core").astype(jnp.int32).reshape(1)
    sems = pltpu.SemaphoreType.DMA

    left = call(
        copies_kernel,
        [(iterate.reshape(2, half, cols), VMEM)],
        bf16(4, 2, half, cols),
        spec=HBM,
        scratch=[sems((4,))],
    )
    left = exchange(left.reshape(8, half, cols), ("y", "core")).reshape(4, 2, half, cols)
    right = gather(iterate, ("z_lo", "core")).reshape(4, 2, rows, cols)

    tile = call(
        gram_kernel,
        [(left, VMEM), (right, VMEM)],
        bf16(4, half, 4 * rows),
        flops=4 * 4 * half * 4 * rows * cols,
    )
    tile, right = lax.optimization_barrier((tile, right))
    own = call(own_kernel, [(core, SMEM), (right, VMEM)], bf16(4 * rows, cols))
    tile, own = lax.optimization_barrier((tile, own))
    piece = total(exchange(tile, "x"))
    for groups in PAIRS:
        piece = piece.astype(jnp.float16)
        piece = total(lax.all_gather(piece, ("z_hi", "core"), axis=0, axis_index_groups=groups))
    gram = gather(piece, ("x", "core")).reshape(4 * rows, 4 * rows)

    packed = bf16(4, rows * cols // LANES, LANES)
    flops = 2 * gram.size * cols
    once = call(first_kernel, [(gram, VMEM), (own, VMEM)], packed, flops=flops)
    once = total(exchange(once, "y"))
    twice = call(
        second_kernel,
        [(gram, VMEM), (lax.all_gather(once.astype(jnp.bfloat16), "z_lo", axis=0), VMEM)],
        packed,
        scratch=[pltpu.VMEM(own.shape, own.dtype)],
        flops=flops,
    )
    return call(
        update_kernel,
        [(iterate, ANY), (once, VMEM), (exchange(twice, "y"), VMEM)],
        bf16(rows, cols),
        scratch=[pltpu.VMEM(iterate.shape, iterate.dtype), sems],
    )


def solution(mesh):
    axes = ("z_lo", "y", "z_hi", "x", "core")
    fine = Mesh(mesh.devices.reshape(4, 4, 4, 4, 2), axes)
    placed = P(axes[:2], axes[2:])
    return jax.shard_map(
        shards, mesh=fine, in_specs=(placed,), out_specs=placed, check_vma=False
    )
```

```python
import math

import jax
import jax.numpy as jnp
from jax import lax
from jax.experimental import pallas as pl
from jax.experimental.pallas import tpu as pltpu
from jax.sharding import Mesh
from jax.sharding import PartitionSpec as P

D = 3584
FF = 18432

coef_linear = 3.4445
coef_cubic = -4.775
coef_quintic = 2.0315

LANES = 128
PAIRS = [[0, 2], [4, 6], [3, 5], [7, 1]], [[2, 4], [6, 0], [1, 3], [5, 7]]
VMEM = pl.BlockSpec(memory_space=pltpu.VMEM)
SMEM = pl.BlockSpec(memory_space=pltpu.SMEM)
HBM = pl.BlockSpec(memory_space=pltpu.HBM)
ANY = pl.BlockSpec(memory_space=pl.ANY)


def call(kernel, operands, output, spec=VMEM, scratch=(), flops=0):
    arrays, in_specs = zip(*operands)
    return pl.pallas_call(
        kernel,
        out_shape=output,
        in_specs=in_specs,
        out_specs=spec,
        scratch_shapes=scratch,
        compiler_params=pltpu.CompilerParams(vmem_limit_bytes=16 * 1024 * 1024),
        cost_estimate=pl.CostEstimate(
            flops=flops,
            bytes_accessed=2 * sum(math.prod(array.shape) for array in (output, *arrays)),
            transcendentals=0,
        ),
    )(*arrays)


def bf16(*shape):
    return jax.ShapeDtypeStruct(shape, jnp.bfloat16)


def dot(lhs, rhs, contract):
    return lax.dot_general(
        lhs, rhs, ((contract[:1], contract[1:]), ((), ())), preferred_element_type=jnp.float32
    )


def copies_kernel(array, out, sems):
    copies = [pltpu.make_async_copy(array, out.at[i], sems.at[i]) for i in range(out.shape[0])]
    for copy in copies:
        copy.start()
    for copy in copies:
        copy.wait()


def gram_kernel(left, right, out):
    blocks, cores, rows, cols = left.shape
    tile = jnp.zeros((blocks * rows, out.shape[-1]), jnp.float32)
    for k in range(cores):
        lhs = left[:, k].reshape(blocks * rows, cols)
        tile += dot(lhs, right[:, k].reshape(out.shape[-1], cols), (1, 1))
    out[...] = tile.astype(out.dtype).reshape(out.shape)


def columns_kernel(core, array, out):
    out[...] = array[:, pl.ds(core[0], 1)].reshape(out.shape)


def pieces(rows, cols):
    whole, rest = cols // LANES, cols % LANES
    for k in range(whole):
        yield slice(0, rows), slice(k * LANES, (k + 1) * LANES), slice(k * rows, (k + 1) * rows), slice(0, LANES)
    each = rows * rest // LANES
    for k in range(LANES // rest if rest else 0):
        columns = slice(k * rest, (k + 1) * rest)
        yield slice(k * each, (k + 1) * each), slice(whole * LANES, cols), slice(whole * rows, whole * rows + each), columns


def product(left, right, out):
    sums = dot(left[...], right[...], (0, 0)).astype(out.dtype)
    rows = sums.shape[0] // out.shape[0]
    for i in range(out.shape[0]):
        block = sums[i * rows : (i + 1) * rows]
        for row, col, packed_row, packed_col in pieces(rows, sums.shape[1]):
            out[i, packed_row, packed_col] = block[row, col]


def first_kernel(core, left, mine, other, out, held):
    blocks, half, _ = mine.shape
    for array, place in ((mine, core[0]), (other, 1 - core[0])):
        for i in range(blocks):
            start = pl.multiple_of(2 * half * i + half * place, 16)
            held[pl.ds(start, half)] = array[i]
    product(left, held, out)


def second_kernel(left, right, out, held):
    rows = held.shape[0] // right.shape[0]
    for i in range(right.shape[0]):
        for row, col, packed_row, packed_col in pieces(rows, held.shape[1]):
            row = slice(i * rows + row.start, i * rows + row.stop)
            held[row, col] = right[i, packed_row, packed_col]
    product(left, held, out)


def update_kernel(iterate, once, parts, out, held, sem):
    fetch = pltpu.make_async_copy(iterate, held, sem)
    fetch.start()
    packed = coef_cubic * once[...]
    packed += coef_quintic * jnp.sum(parts[...].astype(jnp.float32), axis=0)
    fetch.wait()
    for row, col, packed_row, packed_col in pieces(*out.shape):
        step = coef_linear * held[row, col].astype(jnp.float32) + packed[packed_row, packed_col]
        out[row, col] = (0.2 * math.sqrt(max(D, FF)) * step).astype(out.dtype)


def total(parts):
    return jnp.sum(parts.astype(jnp.float32), axis=0)


def gather(array, axes):
    return lax.all_gather(array.astype(jnp.float16), axes, axis=0).astype(jnp.bfloat16)


def exchange(array, axes):
    return lax.all_to_all(array, axes, 0, 0, tiled=True)


def shards(iterate):
    rows, cols = iterate.shape
    half = rows // 2
    core = lax.axis_index("core").astype(jnp.int32).reshape(1)
    sems = pltpu.SemaphoreType.DMA

    right = call(
        copies_kernel,
        [(iterate.reshape(2, half, cols), VMEM)],
        bf16(4, 2, half, cols),
        spec=HBM,
        scratch=[sems((4,))],
    )
    right = exchange(right.reshape(8, half, cols), ("z_lo", "core")).reshape(4, 2, half, cols)
    left = gather(iterate, ("y", "core")).reshape(4, 2, rows, cols)

    tile = call(
        gram_kernel,
        [(right, VMEM), (left, VMEM)],
        bf16(4, half, 4 * rows),
        flops=4 * 4 * half * 4 * rows * cols,
    )
    tile, right = lax.optimization_barrier((tile, right))
    mine, away = (
        call(columns_kernel, [(which, SMEM), (right, VMEM)], bf16(4, half, cols))
        for which in (core, 1 - core)
    )
    tile, mine, away = lax.optimization_barrier((tile, mine, away))
    piece, away = lax.optimization_barrier((total(exchange(tile, "x")), away))
    other = lax.ppermute(away, "core", [(0, 1), (1, 0)])
    for groups in PAIRS:
        piece = piece.astype(jnp.float16)
        piece = total(lax.all_gather(piece, ("z_hi", "core"), axis=0, axis_index_groups=groups))
    gram = gather(piece, ("x", "core")).reshape(4 * rows, 4 * rows)

    packed = bf16(4, rows * cols // LANES, LANES)
    flops = 2 * gram.size * cols
    held = pltpu.VMEM((4 * rows, cols), jnp.bfloat16)
    once = call(
        first_kernel,
        [(core, SMEM), (gram, VMEM), (mine, VMEM), (other, VMEM)],
        packed,
        scratch=[held],
        flops=flops,
    )
    once = total(exchange(once, "y"))
    twice = call(
        second_kernel,
        [(gram, VMEM), (lax.all_gather(once.astype(jnp.bfloat16), "z_lo", axis=0), VMEM)],
        packed,
        scratch=[held],
        flops=flops,
    )
    return call(
        update_kernel,
        [(iterate, ANY), (once, VMEM), (exchange(twice, "y"), VMEM)],
        bf16(rows, cols),
        scratch=[pltpu.VMEM(iterate.shape, iterate.dtype), sems],
    )


def solution(mesh):
    axes = ("z_lo", "y", "z_hi", "x", "core")
    fine = Mesh(mesh.devices.reshape(4, 4, 4, 4, 2), axes)
    placed = P(axes[:2], axes[2:])
    return jax.shard_map(
        shards, mesh=fine, in_specs=(placed,), out_specs=placed, check_vma=False
    )
```

```python
import math

import jax
import jax.numpy as jnp
from jax import lax
from jax.experimental import pallas as pl
from jax.experimental.pallas import tpu as pltpu
from jax.sharding import Mesh
from jax.sharding import PartitionSpec as P

D = 3584
FF = 18432

coef_linear = 3.4445
coef_cubic = -4.775
coef_quintic = 2.0315

LANES = 128
PAIRS = [[0, 2], [4, 6], [3, 5], [7, 1]], [[2, 4], [6, 0], [1, 3], [5, 7]]
GATHERS = [[0, 2], [4, 6], [3, 5], [1, 7]], [[2, 4], [0, 6], [1, 3], [7, 5]]
ORDER = (0, 1, 2, 3), (0, 3, 1, 2)
VMEM = pl.BlockSpec(memory_space=pltpu.VMEM)
SMEM = pl.BlockSpec(memory_space=pltpu.SMEM)
HBM = pl.BlockSpec(memory_space=pltpu.HBM)
ANY = pl.BlockSpec(memory_space=pl.ANY)


def call(kernel, operands, output, spec=VMEM, scratch=(), flops=0):
    arrays, in_specs = zip(*operands)
    return pl.pallas_call(
        kernel,
        out_shape=output,
        in_specs=in_specs,
        out_specs=spec,
        scratch_shapes=scratch,
        compiler_params=pltpu.CompilerParams(vmem_limit_bytes=16 * 1024 * 1024),
        cost_estimate=pl.CostEstimate(
            flops=flops,
            bytes_accessed=2 * sum(math.prod(array.shape) for array in (output, *arrays)),
            transcendentals=0,
        ),
    )(*arrays)


def bf16(*shape):
    return jax.ShapeDtypeStruct(shape, jnp.bfloat16)


def dot(lhs, rhs, rhs_dim):
    return lax.dot_general(
        lhs, rhs, (((1,), (rhs_dim,)), ((), ())), preferred_element_type=jnp.float32
    )


def copies_kernel(array, out, sems):
    copies = [pltpu.make_async_copy(array, out.at[i], sems.at[i]) for i in range(out.shape[0])]
    for copy in copies:
        copy.start()
    for copy in copies:
        copy.wait()


def gram_kernel(left, right, out):
    blocks, cores, rows, cols = left.shape
    tile = jnp.zeros((blocks * rows, out.shape[-1]), jnp.float32)
    for k in range(cores):
        lhs = left[:, k].reshape(blocks * rows, cols)
        tile += dot(lhs, right[:, k].reshape(out.shape[-1], cols), 1)
    out[...] = tile.astype(out.dtype).reshape(out.shape)


def own_kernel(core, right, out):
    out[...] = right[:, pl.ds(core[0], 1)].reshape(out.shape)


def pieces(rows, cols):
    whole, rest = cols // LANES, cols % LANES
    for k in range(whole):
        yield slice(0, rows), slice(k * LANES, (k + 1) * LANES), slice(k * rows, (k + 1) * rows), slice(0, LANES)
    each = rows * rest // LANES
    for k in range(LANES // rest if rest else 0):
        columns = slice(k * rest, (k + 1) * rest)
        yield slice(k * each, (k + 1) * each), slice(whole * LANES, cols), slice(whole * rows, whole * rows + each), columns


def half_pieces(half, rows, cols):
    size = rows // 2
    for row, col, packed_row, packed_col in pieces(rows, cols):
        if row.stop - row.start == rows:
            start = packed_row.start + half * size
            yield col, slice(start, start + size), packed_col
        elif row.start == half * size:
            yield col, packed_row, packed_col


def first_kernel(left, right, out):
    halves, blocks, size, inner = left.shape
    for half in range(halves):
        product = dot(left[half].reshape(blocks * size, inner), right[...], 0).astype(out.dtype)
        for i in range(blocks):
            block = product[i * size : (i + 1) * size]
            for col, packed_row, packed_col in half_pieces(half, 2 * size, product.shape[1]):
                out[ORDER[half][i], packed_row, packed_col] = block[:, col]


def second_kernel(left, right, out, held):
    rows = held.shape[0] // right.shape[0]
    for i in range(right.shape[0]):
        for row, col, packed_row, packed_col in pieces(rows, held.shape[1]):
            row = slice(i * rows + row.start, i * rows + row.stop)
            held[row, col] = right[i, packed_row, packed_col]
    first_kernel(left, held, out)


def update_kernel(iterate, once, parts, out, held, sem):
    fetch = pltpu.make_async_copy(iterate, held, sem)
    fetch.start()
    packed = coef_cubic * once[...]
    packed += coef_quintic * jnp.sum(parts[...].astype(jnp.float32), axis=0)
    fetch.wait()
    for row, col, packed_row, packed_col in pieces(*out.shape):
        step = coef_linear * held[row, col].astype(jnp.float32) + packed[packed_row, packed_col]
        out[row, col] = (0.2 * math.sqrt(max(D, FF)) * step).astype(out.dtype)


def total(parts):
    return jnp.sum(parts.astype(jnp.float32), axis=0)


def gather(array, axes):
    return lax.all_gather(array.astype(jnp.float16), axes, axis=0).astype(jnp.bfloat16)


def exchange(array, axes):
    return lax.all_to_all(array, axes, 0, 0, tiled=True)


def shards(iterate):
    rows, cols = iterate.shape
    half = rows // 2
    core = lax.axis_index("core").astype(jnp.int32).reshape(1)
    sems = pltpu.SemaphoreType.DMA

    left = call(
        copies_kernel,
        [(iterate.reshape(2, half, cols), VMEM)],
        bf16(4, 2, half, cols),
        spec=HBM,
        scratch=[sems((4,))],
    )
    left = exchange(left.reshape(8, half, cols), ("y", "core")).reshape(4, 2, half, cols)
    right = gather(iterate, ("z_lo", "core")).reshape(4, 2, rows, cols)

    tile = call(
        gram_kernel,
        [(left, VMEM), (right, VMEM)],
        bf16(4, half, 4 * rows),
        flops=4 * 4 * half * 4 * rows * cols,
    )
    tile, right = lax.optimization_barrier((tile, right))
    own = call(own_kernel, [(core, SMEM), (right, VMEM)], bf16(4 * rows, cols))
    tile, own = lax.optimization_barrier((tile, own))
    piece = total(exchange(tile, "x"))
    for groups in PAIRS:
        piece = piece.astype(jnp.float16)
        piece = total(lax.all_gather(piece, ("z_hi", "core"), axis=0, axis_index_groups=groups))
    piece = piece.astype(jnp.float16)[None]
    for groups in GATHERS:
        piece = lax.all_gather(
            piece, ("x", "core"), axis=0, tiled=True, axis_index_groups=groups
        )
    gram = lax.all_gather(piece, "core", axis=0).astype(jnp.bfloat16)

    packed = bf16(4, rows * cols // LANES, LANES)
    flops = 2 * gram.size * cols
    once = call(first_kernel, [(gram, VMEM), (own, VMEM)], packed, flops=flops)
    once = total(exchange(once, "y"))
    twice = call(
        second_kernel,
        [(gram, VMEM), (lax.all_gather(once.astype(jnp.bfloat16), "z_lo", axis=0), VMEM)],
        packed,
        scratch=[pltpu.VMEM(own.shape, own.dtype)],
        flops=flops,
    )
    return call(
        update_kernel,
        [(iterate, ANY), (once, VMEM), (exchange(twice, "y"), VMEM)],
        bf16(rows, cols),
        scratch=[pltpu.VMEM(iterate.shape, iterate.dtype), sems],
    )


def solution(mesh):
    axes = ("z_lo", "y", "z_hi", "x", "core")
    fine = Mesh(mesh.devices.reshape(4, 4, 4, 4, 2), axes)
    placed = P(axes[:2], axes[2:])
    return jax.shard_map(
        shards, mesh=fine, in_specs=(placed,), out_specs=placed, check_vma=False
    )
```

```python
import math

import jax
import jax.numpy as jnp
from jax import lax
from jax.experimental import pallas as pl
from jax.experimental.pallas import tpu as pltpu
from jax.sharding import Mesh
from jax.sharding import PartitionSpec as P

D = 3584
FF = 18432

coef_linear = 3.4445
coef_cubic = -4.775
coef_quintic = 2.0315

LANES = 128
PAIRS = [[0, 2], [4, 6], [3, 5], [7, 1]], [[2, 4], [6, 0], [1, 3], [5, 7]]
VMEM = pl.BlockSpec(memory_space=pltpu.VMEM)
SMEM = pl.BlockSpec(memory_space=pltpu.SMEM)
HBM = pl.BlockSpec(memory_space=pltpu.HBM)
ANY = pl.BlockSpec(memory_space=pl.ANY)


def call(kernel, operands, output, spec=VMEM, scratch=(), flops=0):
    arrays, in_specs = zip(*operands)
    return pl.pallas_call(
        kernel,
        out_shape=output,
        in_specs=in_specs,
        out_specs=spec,
        scratch_shapes=scratch,
        compiler_params=pltpu.CompilerParams(vmem_limit_bytes=16 * 1024 * 1024),
        cost_estimate=pl.CostEstimate(
            flops=flops,
            bytes_accessed=2 * sum(math.prod(array.shape) for array in arrays),
            transcendentals=0,
        ),
    )(*arrays)


def bf16(*shape):
    return jax.ShapeDtypeStruct(shape, jnp.bfloat16)


def dot(lhs, rhs, rhs_dim):
    return lax.dot_general(
        lhs, rhs, (((1,), (rhs_dim,)), ((), ())), preferred_element_type=jnp.float32
    )


def pieces(rows, cols):
    whole, rest = cols // LANES, cols % LANES
    for k in range(whole):
        yield slice(0, rows), slice(k * LANES, (k + 1) * LANES), slice(k * rows, (k + 1) * rows), slice(0, LANES)
    each = rows * rest // LANES
    for k in range(LANES // rest if rest else 0):
        columns = slice(k * rest, (k + 1) * rest)
        yield slice(k * each, (k + 1) * each), slice(whole * LANES, cols), slice(whole * rows, whole * rows + each), columns


def unpack(packed, out):
    rows = out.shape[0] // packed.shape[0]
    for i in range(packed.shape[0]):
        for row, col, packed_row, packed_col in pieces(rows, out.shape[1]):
            row = slice(i * rows + row.start, i * rows + row.stop)
            out[row, col] = packed[i, packed_row, packed_col]


def first_kernel(array, out, packed, sems):
    copies = [pltpu.make_async_copy(array, out.at[i], sems.at[i]) for i in range(out.shape[0])]
    for copy in copies:
        copy.start()
    for row, col, packed_row, packed_col in pieces(*array.shape):
        packed[packed_row, packed_col] = array[row, col]
    for copy in copies:
        copy.wait()


def gram_kernel(left, right, out, held):
    blocks, cores, rows, cols = left.shape
    tile = jnp.zeros((blocks * rows, out.shape[-1]), jnp.float32)
    for k in range(cores):
        unpack(right.at[:, k], held.at[k])
        tile += dot(left[:, k].reshape(blocks * rows, cols), held[k], 1)
    out[...] = tile.astype(out.dtype).reshape(out.shape)


def own_kernel(core, right, out):
    out[...] = right[:, pl.ds(core[0], 1)].reshape(out.shape)


def product_kernel(left, right, out, held):
    unpack(right, held)
    product = dot(left[...], held[...], 0).astype(out.dtype)
    rows = product.shape[0] // out.shape[0]
    for i in range(out.shape[0]):
        block = product[i * rows : (i + 1) * rows]
        for row, col, packed_row, packed_col in pieces(rows, product.shape[1]):
            out[i, packed_row, packed_col] = block[row, col]


def update_kernel(iterate, once, parts, out, held, sem):
    fetch = pltpu.make_async_copy(iterate, held, sem)
    fetch.start()
    packed = coef_cubic * once[...]
    packed += coef_quintic * jnp.sum(parts[...].astype(jnp.float32), axis=0)
    fetch.wait()
    for row, col, packed_row, packed_col in pieces(*out.shape):
        step = coef_linear * held[row, col].astype(jnp.float32) + packed[packed_row, packed_col]
        out[row, col] = (0.2 * math.sqrt(max(D, FF)) * step).astype(out.dtype)


def total(parts):
    return jnp.sum(parts.astype(jnp.float32), axis=0)


def gather(array, axes):
    return lax.all_gather(array.astype(jnp.float16), axes, axis=0).astype(jnp.bfloat16)


def exchange(array, axes):
    return lax.all_to_all(array, axes, 0, 0, tiled=True)


def shards(iterate):
    rows, cols = iterate.shape
    half = rows // 2
    core = lax.axis_index("core").astype(jnp.int32).reshape(1)
    sems = pltpu.SemaphoreType.DMA

    packed = rows * cols // LANES
    left, right = call(
        first_kernel,
        [(iterate, VMEM)],
        (bf16(4, rows, cols), bf16(packed, LANES)),
        spec=(HBM, VMEM),
        scratch=[sems((4,))],
    )
    left = exchange(left.reshape(8, half, cols), ("y", "core")).reshape(4, 2, half, cols)
    right = gather(right, ("z_lo", "core")).reshape(4, 2, packed, LANES)

    tile = call(
        gram_kernel,
        [(left, VMEM), (right, VMEM)],
        bf16(4, half, 4 * rows),
        scratch=[pltpu.VMEM((2, 4 * rows, cols), jnp.bfloat16)],
        flops=4 * 4 * half * 4 * rows * cols,
    )
    tile, right = lax.optimization_barrier((tile, right))
    own = call(own_kernel, [(core, SMEM), (right, VMEM)], bf16(4, packed, LANES))
    tile, own = lax.optimization_barrier((tile, own))
    piece = total(exchange(tile, "x"))
    for groups in PAIRS:
        piece = piece.astype(jnp.float16)
        piece = total(lax.all_gather(piece, ("z_hi", "core"), axis=0, axis_index_groups=groups))
    gram = gather(piece, ("x", "core")).reshape(4 * rows, 4 * rows)

    def gram_times(array):
        parts = call(
            product_kernel,
            [(gram, VMEM), (array, VMEM)],
            bf16(4, packed, LANES),
            scratch=[pltpu.VMEM((4 * rows, cols), jnp.bfloat16)],
            flops=2 * gram.size * cols,
        )
        return exchange(parts, "y")

    once = total(gram_times(own))
    twice = gram_times(lax.all_gather(once.astype(jnp.bfloat16), "z_lo", axis=0))
    return call(
        update_kernel,
        [(iterate, ANY), (once, VMEM), (twice, VMEM)],
        bf16(rows, cols),
        scratch=[pltpu.VMEM(iterate.shape, iterate.dtype), sems],
    )


def solution(mesh):
    axes = ("z_lo", "y", "z_hi", "x", "core")
    fine = Mesh(mesh.devices.reshape(4, 4, 4, 4, 2), axes)
    placed = P(axes[:2], axes[2:])
    return jax.shard_map(
        shards, mesh=fine, in_specs=(placed,), out_specs=placed, check_vma=False
    )
```

```python
import math

import jax
import jax.numpy as jnp
from jax import lax
from jax.experimental import pallas as pl
from jax.experimental.pallas import tpu as pltpu
from jax.sharding import Mesh
from jax.sharding import PartitionSpec as P

D = 3584
FF = 18432

coef_linear = 3.4445
coef_cubic = -4.775
coef_quintic = 2.0315

LANES = 128
PAIRS = [[0, 2], [4, 6], [3, 5], [7, 1]], [[2, 4], [6, 0], [1, 3], [5, 7]]
VMEM = pl.BlockSpec(memory_space=pltpu.VMEM)
SMEM = pl.BlockSpec(memory_space=pltpu.SMEM)
HBM = pl.BlockSpec(memory_space=pltpu.HBM)
ANY = pl.BlockSpec(memory_space=pl.ANY)


def call(kernel, operands, output, spec=VMEM, scratch=(), flops=0, vmem=16):
    arrays, in_specs = zip(*operands)
    return pl.pallas_call(
        kernel,
        out_shape=output,
        in_specs=in_specs,
        out_specs=spec,
        scratch_shapes=scratch,
        compiler_params=pltpu.CompilerParams(vmem_limit_bytes=vmem * 1024 * 1024),
        cost_estimate=pl.CostEstimate(
            flops=flops,
            bytes_accessed=2 * sum(math.prod(array.shape) for array in arrays),
            transcendentals=0,
        ),
    )(*arrays)


def bf16(*shape):
    return jax.ShapeDtypeStruct(shape, jnp.bfloat16)


def dot(lhs, rhs, rhs_dim):
    return lax.dot_general(
        lhs, rhs, (((1,), (rhs_dim,)), ((), ())), preferred_element_type=jnp.float32
    )


def pieces(rows, cols):
    whole, rest = cols // LANES, cols % LANES
    for k in range(whole):
        yield slice(0, rows), slice(k * LANES, (k + 1) * LANES), slice(k * rows, (k + 1) * rows), slice(0, LANES)
    each = rows * rest // LANES
    for k in range(LANES // rest if rest else 0):
        columns = slice(k * rest, (k + 1) * rest)
        yield slice(k * each, (k + 1) * each), slice(whole * LANES, cols), slice(whole * rows, whole * rows + each), columns


def unpack(packed, out):
    rows = out.shape[0] // packed.shape[0]
    for i in range(packed.shape[0]):
        for row, col, packed_row, packed_col in pieces(rows, out.shape[1]):
            row = slice(i * rows + row.start, i * rows + row.stop)
            out[row, col] = packed[i, packed_row, packed_col]


def first_kernel(array, out, packed, held, sems):
    count = out.shape[0]
    fetch = pltpu.make_async_copy(array, held, sems.at[count])
    fetch.start()
    fetch.wait()
    copies = [pltpu.make_async_copy(held, out.at[i], sems.at[i]) for i in range(count)]
    for copy in copies:
        copy.start()
    for row, col, packed_row, packed_col in pieces(*held.shape):
        packed[packed_row, packed_col] = held[row, col]
    for copy in copies:
        copy.wait()


def gram_kernel(left, right, out, held):
    blocks, cores, rows, cols = left.shape
    tile = jnp.zeros((blocks * rows, out.shape[-1]), jnp.float32)
    for k in range(cores):
        unpack(right.at[:, k], held.at[k])
        tile += dot(left[:, k].reshape(blocks * rows, cols), held[k], 1)
    out[...] = tile.astype(out.dtype).reshape(out.shape)


def own_kernel(core, right, out):
    out[...] = right[:, pl.ds(core[0], 1)].reshape(out.shape)


def product_kernel(left, right, out, held):
    unpack(right, held)
    product = dot(left[...], held[...], 0).astype(out.dtype)
    rows = product.shape[0] // out.shape[0]
    for i in range(out.shape[0]):
        block = product[i * rows : (i + 1) * rows]
        for row, col, packed_row, packed_col in pieces(rows, product.shape[1]):
            out[i, packed_row, packed_col] = block[row, col]


def update_kernel(iterate, once, parts, out, held, sem):
    fetch = pltpu.make_async_copy(iterate, held, sem)
    fetch.start()
    packed = coef_cubic * once[...]
    packed += coef_quintic * jnp.sum(parts[...].astype(jnp.float32), axis=0)
    fetch.wait()
    for row, col, packed_row, packed_col in pieces(*out.shape):
        step = coef_linear * held[row, col].astype(jnp.float32) + packed[packed_row, packed_col]
        out[row, col] = (0.2 * math.sqrt(max(D, FF)) * step).astype(out.dtype)


def total(parts):
    return jnp.sum(parts.astype(jnp.float32), axis=0)


def gather(array, axes):
    return lax.all_gather(array.astype(jnp.float16), axes, axis=0).astype(jnp.bfloat16)


def exchange(array, axes):
    return lax.all_to_all(array, axes, 0, 0, tiled=True)


def shards(iterate):
    rows, cols = iterate.shape
    half = rows // 2
    core = lax.axis_index("core").astype(jnp.int32).reshape(1)
    sems = pltpu.SemaphoreType.DMA

    packed = rows * cols // LANES
    left, right = call(
        first_kernel,
        [(iterate, ANY)],
        (bf16(4, rows, cols), bf16(packed, LANES)),
        spec=(HBM, VMEM),
        scratch=[pltpu.VMEM(iterate.shape, iterate.dtype), sems((5,))],
        vmem=56,
    )
    left = exchange(left.reshape(8, half, cols), ("y", "core")).reshape(4, 2, half, cols)
    right = gather(right, ("z_lo", "core")).reshape(4, 2, packed, LANES)

    tile = call(
        gram_kernel,
        [(left, VMEM), (right, VMEM)],
        bf16(4, half, 4 * rows),
        scratch=[pltpu.VMEM((2, 4 * rows, cols), jnp.bfloat16)],
        flops=4 * 4 * half * 4 * rows * cols,
    )
    tile, right = lax.optimization_barrier((tile, right))
    own = call(own_kernel, [(core, SMEM), (right, VMEM)], bf16(4, packed, LANES))
    tile, own = lax.optimization_barrier((tile, own))
    piece = total(exchange(tile, "x"))
    for groups in PAIRS:
        piece = piece.astype(jnp.float16)
        piece = total(lax.all_gather(piece, ("z_hi", "core"), axis=0, axis_index_groups=groups))
    gram = gather(piece, ("x", "core")).reshape(4 * rows, 4 * rows)

    def gram_times(array):
        parts = call(
            product_kernel,
            [(gram, VMEM), (array, VMEM)],
            bf16(4, packed, LANES),
            scratch=[pltpu.VMEM((4 * rows, cols), jnp.bfloat16)],
            flops=2 * gram.size * cols,
        )
        return exchange(parts, "y")

    once = total(gram_times(own))
    twice = gram_times(lax.all_gather(once.astype(jnp.bfloat16), "z_lo", axis=0))
    return call(
        update_kernel,
        [(iterate, ANY), (once, VMEM), (twice, VMEM)],
        bf16(rows, cols),
        scratch=[pltpu.VMEM(iterate.shape, iterate.dtype), sems],
    )


def solution(mesh):
    axes = ("z_lo", "y", "z_hi", "x", "core")
    fine = Mesh(mesh.devices.reshape(4, 4, 4, 4, 2), axes)
    placed = P(axes[:2], axes[2:])
    return jax.shard_map(
        shards, mesh=fine, in_specs=(placed,), out_specs=placed, check_vma=False
    )
```

```python
import math

import jax
import jax.numpy as jnp
from jax import lax
from jax.experimental import pallas as pl
from jax.experimental.pallas import tpu as pltpu
from jax.sharding import Mesh
from jax.sharding import PartitionSpec as P

D = 3584
FF = 18432

coef_linear = 3.4445
coef_cubic = -4.775
coef_quintic = 2.0315

LANES = 128
PAIRS = [[0, 2], [4, 6], [3, 5], [7, 1]], [[2, 4], [6, 0], [1, 3], [5, 7]]
VMEM = pl.BlockSpec(memory_space=pltpu.VMEM)
SMEM = pl.BlockSpec(memory_space=pltpu.SMEM)
HBM = pl.BlockSpec(memory_space=pltpu.HBM)
ANY = pl.BlockSpec(memory_space=pl.ANY)


def call(kernel, operands, output, spec=VMEM, scratch=(), flops=0):
    arrays, in_specs = zip(*operands)
    return pl.pallas_call(
        kernel,
        out_shape=output,
        in_specs=in_specs,
        out_specs=spec,
        scratch_shapes=scratch,
        compiler_params=pltpu.CompilerParams(vmem_limit_bytes=16 * 1024 * 1024),
        cost_estimate=pl.CostEstimate(
            flops=flops,
            bytes_accessed=2 * sum(math.prod(array.shape) for array in arrays),
            transcendentals=0,
        ),
    )(*arrays)


def bf16(*shape):
    return jax.ShapeDtypeStruct(shape, jnp.bfloat16)


def dot(lhs, rhs, rhs_dim):
    return lax.dot_general(
        lhs, rhs, (((1,), (rhs_dim,)), ((), ())), preferred_element_type=jnp.float32
    )


def pieces(rows, cols):
    whole, rest = cols // LANES, cols % LANES
    for k in range(whole):
        yield slice(0, rows), slice(k * LANES, (k + 1) * LANES), slice(k * rows, (k + 1) * rows), slice(0, LANES)
    each = rows * rest // LANES
    for k in range(LANES // rest if rest else 0):
        columns = slice(k * rest, (k + 1) * rest)
        yield slice(k * each, (k + 1) * each), slice(whole * LANES, cols), slice(whole * rows, whole * rows + each), columns


def unpack(packed, out):
    rows = out.shape[0] // packed.shape[0]
    for i in range(packed.shape[0]):
        for row, col, packed_row, packed_col in pieces(rows, out.shape[1]):
            row = slice(i * rows + row.start, i * rows + row.stop)
            out[row, col] = packed[i, packed_row, packed_col]


def first_kernel(array, out, packed, sems):
    copies = [pltpu.make_async_copy(array, out.at[i], sems.at[i]) for i in range(out.shape[0])]
    for copy in copies:
        copy.start()
    for row, col, packed_row, packed_col in pieces(*array.shape):
        packed[packed_row, packed_col] = array[row, col]
    for copy in copies:
        copy.wait()


def gram_kernel(left, right, out, held):
    blocks, cores, rows, cols = left.shape
    tile = jnp.zeros((blocks * rows, out.shape[-1]), jnp.float32)
    for k in range(cores):
        unpack(right.at[k], held.at[k])
        tile += dot(left[:, k].reshape(blocks * rows, cols), held[k], 1)
    out[...] = tile.astype(out.dtype).reshape(out.shape)


def own_kernel(core, right, out):
    out[...] = right[core[0]]


def product_kernel(left, right, out, held):
    unpack(right, held)
    product = dot(left[...], held[...], 0).astype(out.dtype)
    rows = product.shape[0] // out.shape[0]
    for i in range(out.shape[0]):
        block = product[i * rows : (i + 1) * rows]
        for row, col, packed_row, packed_col in pieces(rows, product.shape[1]):
            out[i, packed_row, packed_col] = block[row, col]


def update_kernel(iterate, once, parts, out, held, sem):
    fetch = pltpu.make_async_copy(iterate, held, sem)
    fetch.start()
    packed = coef_cubic * once[...]
    packed += coef_quintic * jnp.sum(parts[...].astype(jnp.float32), axis=0)
    fetch.wait()
    for row, col, packed_row, packed_col in pieces(*out.shape):
        step = coef_linear * held[row, col].astype(jnp.float32) + packed[packed_row, packed_col]
        out[row, col] = (0.2 * math.sqrt(max(D, FF)) * step).astype(out.dtype)


def total(parts):
    return jnp.sum(parts.astype(jnp.float32), axis=0)


def gather(array, axis):
    array = lax.all_gather(array.astype(jnp.float16), axis, axis=0)
    return lax.all_gather(array, "core", axis=0).astype(jnp.bfloat16)


def exchange(array, axes):
    return lax.all_to_all(array, axes, 0, 0, tiled=True)


def shards(iterate):
    rows, cols = iterate.shape
    half = rows // 2
    core = lax.axis_index("core").astype(jnp.int32).reshape(1)
    sems = pltpu.SemaphoreType.DMA

    packed = rows * cols // LANES
    left, right = call(
        first_kernel,
        [(iterate, VMEM)],
        (bf16(4, rows, cols), bf16(packed, LANES)),
        spec=(HBM, VMEM),
        scratch=[sems((4,))],
    )
    left = exchange(left.reshape(8, half, cols), ("y", "core")).reshape(4, 2, half, cols)
    right = gather(right, "z_lo")

    tile = call(
        gram_kernel,
        [(left, VMEM), (right, VMEM)],
        bf16(4, half, 4 * rows),
        scratch=[pltpu.VMEM((2, 4 * rows, cols), jnp.bfloat16)],
        flops=4 * 4 * half * 4 * rows * cols,
    )
    tile, right = lax.optimization_barrier((tile, right))
    own = call(own_kernel, [(core, SMEM), (right, VMEM)], bf16(4, packed, LANES))
    tile, own = lax.optimization_barrier((tile, own))
    piece = total(exchange(tile, "x"))
    for groups in PAIRS:
        piece = piece.astype(jnp.float16)
        piece = total(lax.all_gather(piece, ("z_hi", "core"), axis=0, axis_index_groups=groups))
    gram = gather(piece, "x").transpose(1, 0, 2, 3).reshape(4 * rows, 4 * rows)

    def gram_times(array):
        parts = call(
            product_kernel,
            [(gram, VMEM), (array, VMEM)],
            bf16(4, packed, LANES),
            scratch=[pltpu.VMEM((4 * rows, cols), jnp.bfloat16)],
            flops=2 * gram.size * cols,
        )
        return exchange(parts, "y")

    once = total(gram_times(own))
    twice = gram_times(lax.all_gather(once.astype(jnp.bfloat16), "z_lo", axis=0))
    return call(
        update_kernel,
        [(iterate, ANY), (once, VMEM), (twice, VMEM)],
        bf16(rows, cols),
        scratch=[pltpu.VMEM(iterate.shape, iterate.dtype), sems],
    )


def solution(mesh):
    axes = ("z_lo", "y", "z_hi", "x", "core")
    fine = Mesh(mesh.devices.reshape(4, 4, 4, 4, 2), axes)
    placed = P(axes[:2], axes[2:])
    return jax.shard_map(
        shards, mesh=fine, in_specs=(placed,), out_specs=placed, check_vma=False
    )
```

```python
import math

import jax
import jax.numpy as jnp
from jax import lax
from jax.experimental import pallas as pl
from jax.experimental.pallas import tpu as pltpu
from jax.sharding import Mesh
from jax.sharding import PartitionSpec as P

D = 3584
FF = 18432

coef_linear = 3.4445
coef_cubic = -4.775
coef_quintic = 2.0315

LANES = 128
PAIRS = [[2, 4], [6, 0], [1, 3], [5, 7]], [[0, 2], [4, 6], [3, 5], [7, 1]]
VMEM = pl.BlockSpec(memory_space=pltpu.VMEM)
SMEM = pl.BlockSpec(memory_space=pltpu.SMEM)
HBM = pl.BlockSpec(memory_space=pltpu.HBM)
ANY = pl.BlockSpec(memory_space=pl.ANY)


def call(kernel, operands, output, spec=VMEM, scratch=(), flops=0):
    arrays, in_specs = zip(*operands)
    return pl.pallas_call(
        kernel,
        out_shape=output,
        in_specs=in_specs,
        out_specs=spec,
        scratch_shapes=scratch,
        compiler_params=pltpu.CompilerParams(vmem_limit_bytes=16 * 1024 * 1024),
        cost_estimate=pl.CostEstimate(
            flops=flops,
            bytes_accessed=2 * sum(math.prod(array.shape) for array in arrays),
            transcendentals=0,
        ),
    )(*arrays)


def bf16(*shape):
    return jax.ShapeDtypeStruct(shape, jnp.bfloat16)


def dot(lhs, rhs, rhs_dim):
    return lax.dot_general(
        lhs, rhs, (((1,), (rhs_dim,)), ((), ())), preferred_element_type=jnp.float32
    )


def pieces(rows, cols):
    whole, rest = cols // LANES, cols % LANES
    for k in range(whole):
        yield slice(0, rows), slice(k * LANES, (k + 1) * LANES), slice(k * rows, (k + 1) * rows), slice(0, LANES)
    each = rows * rest // LANES
    for k in range(LANES // rest if rest else 0):
        columns = slice(k * rest, (k + 1) * rest)
        yield slice(k * each, (k + 1) * each), slice(whole * LANES, cols), slice(whole * rows, whole * rows + each), columns


def unpack(packed, out):
    rows = out.shape[0] // packed.shape[0]
    for i in range(packed.shape[0]):
        for row, col, packed_row, packed_col in pieces(rows, out.shape[1]):
            row = slice(i * rows + row.start, i * rows + row.stop)
            out[row, col] = packed[i, packed_row, packed_col]


def first_kernel(array, out, packed, sems):
    copies = [pltpu.make_async_copy(array, out.at[i], sems.at[i]) for i in range(out.shape[0])]
    for copy in copies:
        copy.start()
    for row, col, packed_row, packed_col in pieces(*array.shape):
        packed[packed_row, packed_col] = array[row, col]
    for copy in copies:
        copy.wait()


def gram_kernel(left, right, out, held):
    blocks, cores, rows, cols = left.shape
    tile = jnp.zeros((blocks * rows, out.shape[-1]), jnp.float32)
    for k in range(cores):
        unpack(right.at[:, k], held.at[k])
        tile += dot(left[:, k].reshape(blocks * rows, cols), held[k], 1)
    out[...] = tile.astype(out.dtype).reshape(out.shape)


def own_kernel(core, right, out):
    out[...] = right[:, pl.ds(core[0], 1)].reshape(out.shape)


def product_kernel(left, right, out, held):
    unpack(right, held)
    product = dot(left[...], held[...], 0).astype(out.dtype)
    rows = product.shape[0] // out.shape[0]
    for i in range(out.shape[0]):
        block = product[i * rows : (i + 1) * rows]
        for row, col, packed_row, packed_col in pieces(rows, product.shape[1]):
            out[i, packed_row, packed_col] = block[row, col]


def update_kernel(iterate, once, parts, out, held, sem):
    fetch = pltpu.make_async_copy(iterate, held, sem)
    fetch.start()
    packed = coef_cubic * once[...]
    packed += coef_quintic * jnp.sum(parts[...].astype(jnp.float32), axis=0)
    fetch.wait()
    for row, col, packed_row, packed_col in pieces(*out.shape):
        step = coef_linear * held[row, col].astype(jnp.float32) + packed[packed_row, packed_col]
        out[row, col] = (0.2 * math.sqrt(max(D, FF)) * step).astype(out.dtype)


def total(parts):
    return jnp.sum(parts.astype(jnp.float32), axis=0)


def gather(array, axes):
    return lax.all_gather(array.astype(jnp.float16), axes, axis=0).astype(jnp.bfloat16)


def exchange(array, axes):
    return lax.all_to_all(array, axes, 0, 0, tiled=True)


def shards(iterate):
    rows, cols = iterate.shape
    half = rows // 2
    core = lax.axis_index("core").astype(jnp.int32).reshape(1)
    sems = pltpu.SemaphoreType.DMA

    packed = rows * cols // LANES
    left, right = call(
        first_kernel,
        [(iterate, VMEM)],
        (bf16(4, rows, cols), bf16(packed, LANES)),
        spec=(HBM, VMEM),
        scratch=[sems((4,))],
    )
    left = exchange(left.reshape(8, half, cols), ("y", "core")).reshape(4, 2, half, cols)
    right = gather(right, ("z_lo", "core")).reshape(4, 2, packed, LANES)

    tile = call(
        gram_kernel,
        [(left, VMEM), (right, VMEM)],
        bf16(4, half, 4 * rows),
        scratch=[pltpu.VMEM((2, 4 * rows, cols), jnp.bfloat16)],
        flops=4 * 4 * half * 4 * rows * cols,
    )
    tile, right = lax.optimization_barrier((tile, right))
    own = call(own_kernel, [(core, SMEM), (right, VMEM)], bf16(4, packed, LANES))
    tile, own = lax.optimization_barrier((tile, own))
    piece = total(exchange(tile, "x"))
    for groups in PAIRS:
        piece = piece.astype(jnp.float16)
        piece = total(lax.all_gather(piece, ("z_hi", "core"), axis=0, axis_index_groups=groups))
    gram = gather(piece, ("x", "core")).reshape(4 * rows, 4 * rows)

    def gram_times(array):
        parts = call(
            product_kernel,
            [(gram, VMEM), (array, VMEM)],
            bf16(4, packed, LANES),
            scratch=[pltpu.VMEM((4 * rows, cols), jnp.bfloat16)],
            flops=2 * gram.size * cols,
        )
        return exchange(parts, "y")

    once = total(gram_times(own))
    twice = gram_times(lax.all_gather(once.astype(jnp.bfloat16), "z_lo", axis=0))
    return call(
        update_kernel,
        [(iterate, ANY), (once, VMEM), (twice, VMEM)],
        bf16(rows, cols),
        scratch=[pltpu.VMEM(iterate.shape, iterate.dtype), sems],
    )


def solution(mesh):
    axes = ("z_lo", "y", "z_hi", "x", "core")
    fine = Mesh(mesh.devices.reshape(4, 4, 4, 4, 2), axes)
    placed = P(axes[:2], axes[2:])
    return jax.shard_map(
        shards, mesh=fine, in_specs=(placed,), out_specs=placed, check_vma=False
    )
```

```python
import math

import jax
import jax.numpy as jnp
from jax import lax
from jax.experimental import pallas as pl
from jax.experimental.pallas import tpu as pltpu
from jax.sharding import Mesh
from jax.sharding import PartitionSpec as P

D = 3584
FF = 18432

coef_linear = 3.4445
coef_cubic = -4.775
coef_quintic = 2.0315

LANES = 128
PAIRS = [[0, 2], [4, 6], [3, 5], [7, 1]], [[2, 4], [6, 0], [1, 3], [5, 7]]
VMEM = pl.BlockSpec(memory_space=pltpu.VMEM)
SMEM = pl.BlockSpec(memory_space=pltpu.SMEM)
ANY = pl.BlockSpec(memory_space=pl.ANY)


def call(kernel, operands, output, spec=VMEM, scratch=(), flops=0):
    arrays, in_specs = zip(*operands)
    return pl.pallas_call(
        kernel,
        out_shape=output,
        in_specs=in_specs,
        out_specs=spec,
        scratch_shapes=scratch,
        compiler_params=pltpu.CompilerParams(vmem_limit_bytes=16 * 1024 * 1024),
        cost_estimate=pl.CostEstimate(
            flops=flops,
            bytes_accessed=2 * sum(math.prod(array.shape) for array in arrays),
            transcendentals=0,
        ),
    )(*arrays)


def bf16(*shape):
    return jax.ShapeDtypeStruct(shape, jnp.bfloat16)


def dot(lhs, rhs, rhs_dim):
    return lax.dot_general(
        lhs, rhs, (((1,), (rhs_dim,)), ((), ())), preferred_element_type=jnp.float32
    )


def pieces(rows, cols):
    whole, rest = cols // LANES, cols % LANES
    for k in range(whole):
        yield slice(0, rows), slice(k * LANES, (k + 1) * LANES), slice(k * rows, (k + 1) * rows), slice(0, LANES)
    each = rows * rest // LANES
    for k in range(LANES // rest if rest else 0):
        columns = slice(k * rest, (k + 1) * rest)
        yield slice(k * each, (k + 1) * each), slice(whole * LANES, cols), slice(whole * rows, whole * rows + each), columns


def unpack(packed, out):
    rows = out.shape[0] // packed.shape[0]
    for i in range(packed.shape[0]):
        for row, col, packed_row, packed_col in pieces(rows, out.shape[1]):
            row = slice(i * rows + row.start, i * rows + row.stop)
            out[row, col] = packed[i, packed_row, packed_col]


def pack_kernel(array, packed):
    for row, col, packed_row, packed_col in pieces(*array.shape):
        packed[packed_row, packed_col] = array[row, col]


def gram_kernel(left, right, out, held):
    blocks, cores, rows, cols = left.shape
    tile = jnp.zeros((blocks * rows, out.shape[-1]), jnp.float32)
    for k in range(cores):
        unpack(right.at[:, k], held.at[k])
        tile += dot(left[:, k].reshape(blocks * rows, cols), held[k], 1)
    out[...] = tile.astype(out.dtype).reshape(out.shape)


def own_kernel(core, right, out):
    out[...] = right[:, pl.ds(core[0], 1)].reshape(out.shape)


def product_kernel(left, right, out, held):
    unpack(right, held)
    product = dot(left[...], held[...], 0).astype(out.dtype)
    rows = product.shape[0] // out.shape[0]
    for i in range(out.shape[0]):
        block = product[i * rows : (i + 1) * rows]
        for row, col, packed_row, packed_col in pieces(rows, product.shape[1]):
            out[i, packed_row, packed_col] = block[row, col]


def update_kernel(iterate, once, parts, out, held, sem):
    fetch = pltpu.make_async_copy(iterate, held, sem)
    fetch.start()
    packed = coef_cubic * once[...]
    packed += coef_quintic * jnp.sum(parts[...].astype(jnp.float32), axis=0)
    fetch.wait()
    for row, col, packed_row, packed_col in pieces(*out.shape):
        step = coef_linear * held[row, col].astype(jnp.float32) + packed[packed_row, packed_col]
        out[row, col] = (0.2 * math.sqrt(max(D, FF)) * step).astype(out.dtype)


def total(parts):
    return jnp.sum(parts.astype(jnp.float32), axis=0)


def gather(array, axes):
    return lax.all_gather(array.astype(jnp.float16), axes, axis=0).astype(jnp.bfloat16)


def exchange(array, axes):
    return lax.all_to_all(array, axes, 0, 0, tiled=True)


def shards(iterate):
    rows, cols = iterate.shape
    half = rows // 2
    core = lax.axis_index("core").astype(jnp.int32).reshape(1)
    sems = pltpu.SemaphoreType.DMA

    packed = rows * cols // LANES
    left = jnp.broadcast_to(iterate, (4, rows, cols))
    left = exchange(left.reshape(8, half, cols), ("y", "core")).reshape(4, 2, half, cols)
    right = call(pack_kernel, [(iterate, VMEM)], bf16(packed, LANES))
    right = gather(right, ("z_lo", "core")).reshape(4, 2, packed, LANES)

    tile = call(
        gram_kernel,
        [(left, VMEM), (right, VMEM)],
        bf16(4, half, 4 * rows),
        scratch=[pltpu.VMEM((2, 4 * rows, cols), jnp.bfloat16)],
        flops=4 * 4 * half * 4 * rows * cols,
    )
    tile, right = lax.optimization_barrier((tile, right))
    own = call(own_kernel, [(core, SMEM), (right, VMEM)], bf16(4, packed, LANES))
    tile, own = lax.optimization_barrier((tile, own))
    piece = total(exchange(tile, "x"))
    for groups in PAIRS:
        piece = piece.astype(jnp.float16)
        piece = total(lax.all_gather(piece, ("z_hi", "core"), axis=0, axis_index_groups=groups))
    gram = gather(piece, ("x", "core")).reshape(4 * rows, 4 * rows)

    def gram_times(array):
        parts = call(
            product_kernel,
            [(gram, VMEM), (array, VMEM)],
            bf16(4, packed, LANES),
            scratch=[pltpu.VMEM((4 * rows, cols), jnp.bfloat16)],
            flops=2 * gram.size * cols,
        )
        return exchange(parts, "y")

    once = total(gram_times(own))
    twice = gram_times(lax.all_gather(once.astype(jnp.bfloat16), "z_lo", axis=0))
    return call(
        update_kernel,
        [(iterate, ANY), (once, VMEM), (twice, VMEM)],
        bf16(rows, cols),
        scratch=[pltpu.VMEM(iterate.shape, iterate.dtype), sems],
    )


def solution(mesh):
    axes = ("z_lo", "y", "z_hi", "x", "core")
    fine = Mesh(mesh.devices.reshape(4, 4, 4, 4, 2), axes)
    placed = P(axes[:2], axes[2:])
    return jax.shard_map(
        shards, mesh=fine, in_specs=(placed,), out_specs=placed, check_vma=False
    )
```

```python
import math

import jax
import jax.numpy as jnp
from jax import lax
from jax.experimental import pallas as pl
from jax.experimental.pallas import tpu as pltpu
from jax.sharding import Mesh
from jax.sharding import PartitionSpec as P

D = 3584
FF = 18432

coef_linear = 3.4445
coef_cubic = -4.775
coef_quintic = 2.0315

LANES = 128
PAIRS = [[0, 2], [4, 6], [3, 5], [7, 1]], [[2, 4], [6, 0], [1, 3], [5, 7]]
VMEM = pl.BlockSpec(memory_space=pltpu.VMEM)
SMEM = pl.BlockSpec(memory_space=pltpu.SMEM)
ANY = pl.BlockSpec(memory_space=pl.ANY)
HBM = pl.BlockSpec(memory_space=pltpu.HBM)


def call(kernel, operands, output, spec=VMEM, scratch=(), flops=0, vmem=16):
    arrays, in_specs = zip(*operands)
    return pl.pallas_call(
        kernel,
        out_shape=output,
        in_specs=in_specs,
        out_specs=spec,
        scratch_shapes=scratch,
        compiler_params=pltpu.CompilerParams(vmem_limit_bytes=vmem * 1024 * 1024),
        cost_estimate=pl.CostEstimate(
            flops=flops,
            bytes_accessed=2 * sum(math.prod(array.shape) for array in arrays),
            transcendentals=0,
        ),
    )(*arrays)


def bf16(*shape):
    return jax.ShapeDtypeStruct(shape, jnp.bfloat16)


def dot(lhs, rhs, rhs_dim):
    return lax.dot_general(
        lhs, rhs, (((1,), (rhs_dim,)), ((), ())), preferred_element_type=jnp.float32
    )


def pieces(rows, cols):
    whole, rest = cols // LANES, cols % LANES
    for k in range(whole):
        yield slice(0, rows), slice(k * LANES, (k + 1) * LANES), slice(k * rows, (k + 1) * rows), slice(0, LANES)
    each = rows * rest // LANES
    for k in range(LANES // rest if rest else 0):
        columns = slice(k * rest, (k + 1) * rest)
        yield slice(k * each, (k + 1) * each), slice(whole * LANES, cols), slice(whole * rows, whole * rows + each), columns


def unpack(packed, out):
    rows = out.shape[0] // packed.shape[0]
    for i in range(packed.shape[0]):
        for row, col, packed_row, packed_col in pieces(rows, out.shape[1]):
            row = slice(i * rows + row.start, i * rows + row.stop)
            out[row, col] = packed[i, packed_row, packed_col]


def copies_kernel(array, out, held, sems):
    rows, count = array.shape[0] // 2, out.shape[0]
    halves = [pl.ds(half * rows, rows) for half in range(2)]
    fetches = [
        pltpu.make_async_copy(array.at[half], held.at[half], sems.at[count, k])
        for k, half in enumerate(halves)
    ]
    copies = [
        [pltpu.make_async_copy(held.at[half], out.at[i, half], sems.at[i, k]) for i in range(count)]
        for k, half in enumerate(halves)
    ]
    for fetch in fetches:
        fetch.start()
    for fetch, sends in zip(fetches, copies):
        fetch.wait()
        for copy in sends:
            copy.start()
    for copy in copies[0] + copies[1]:
        copy.wait()


def pack_kernel(array, packed):
    for row, col, packed_row, packed_col in pieces(*array.shape):
        packed[packed_row, packed_col] = array[row, col]


def gram_kernel(left, right, out, held):
    blocks, cores, rows, cols = left.shape
    tile = jnp.zeros((blocks * rows, out.shape[-1]), jnp.float32)
    for k in range(cores):
        unpack(right.at[:, k], held.at[k])
        tile += dot(left[:, k].reshape(blocks * rows, cols), held[k], 1)
    out[...] = tile.astype(out.dtype).reshape(out.shape)


def own_kernel(core, right, out):
    out[...] = right[:, pl.ds(core[0], 1)].reshape(out.shape)


def product_kernel(left, right, out, held):
    unpack(right, held)
    product = dot(left[...], held[...], 0).astype(out.dtype)
    rows = product.shape[0] // out.shape[0]
    for i in range(out.shape[0]):
        block = product[i * rows : (i + 1) * rows]
        for row, col, packed_row, packed_col in pieces(rows, product.shape[1]):
            out[i, packed_row, packed_col] = block[row, col]


def update_kernel(iterate, once, parts, out, held, sem):
    fetch = pltpu.make_async_copy(iterate, held, sem)
    fetch.start()
    packed = coef_cubic * once[...]
    packed += coef_quintic * jnp.sum(parts[...].astype(jnp.float32), axis=0)
    fetch.wait()
    for row, col, packed_row, packed_col in pieces(*out.shape):
        step = coef_linear * held[row, col].astype(jnp.float32) + packed[packed_row, packed_col]
        out[row, col] = (0.2 * math.sqrt(max(D, FF)) * step).astype(out.dtype)


def total(parts):
    return jnp.sum(parts.astype(jnp.float32), axis=0)


def gather(array, axes):
    return lax.all_gather(array.astype(jnp.float16), axes, axis=0).astype(jnp.bfloat16)


def exchange(array, axes):
    return lax.all_to_all(array, axes, 0, 0, tiled=True)


def shards(iterate):
    rows, cols = iterate.shape
    half = rows // 2
    core = lax.axis_index("core").astype(jnp.int32).reshape(1)
    sems = pltpu.SemaphoreType.DMA

    packed = rows * cols // LANES
    left = call(
        copies_kernel,
        [(iterate, ANY)],
        bf16(4, rows, cols),
        spec=HBM,
        scratch=[pltpu.VMEM(iterate.shape, iterate.dtype), sems((5, 2))],
        vmem=56,
    )
    left = exchange(left.reshape(8, half, cols), ("y", "core")).reshape(4, 2, half, cols)
    right = call(pack_kernel, [(iterate, VMEM)], bf16(packed, LANES))
    right = gather(right, ("z_lo", "core")).reshape(4, 2, packed, LANES)

    tile = call(
        gram_kernel,
        [(left, VMEM), (right, VMEM)],
        bf16(4, half, 4 * rows),
        scratch=[pltpu.VMEM((2, 4 * rows, cols), jnp.bfloat16)],
        flops=4 * 4 * half * 4 * rows * cols,
    )
    tile, right = lax.optimization_barrier((tile, right))
    own = call(own_kernel, [(core, SMEM), (right, VMEM)], bf16(4, packed, LANES))
    tile, own = lax.optimization_barrier((tile, own))
    piece = total(exchange(tile, "x"))
    for groups in PAIRS:
        piece = piece.astype(jnp.float16)
        piece = total(lax.all_gather(piece, ("z_hi", "core"), axis=0, axis_index_groups=groups))
    gram = gather(piece, ("x", "core")).reshape(4 * rows, 4 * rows)

    def gram_times(array):
        parts = call(
            product_kernel,
            [(gram, VMEM), (array, VMEM)],
            bf16(4, packed, LANES),
            scratch=[pltpu.VMEM((4 * rows, cols), jnp.bfloat16)],
            flops=2 * gram.size * cols,
        )
        return exchange(parts, "y")

    once = total(gram_times(own))
    twice = gram_times(lax.all_gather(once.astype(jnp.bfloat16), "z_lo", axis=0))
    return call(
        update_kernel,
        [(iterate, ANY), (once, VMEM), (twice, VMEM)],
        bf16(rows, cols),
        scratch=[pltpu.VMEM(iterate.shape, iterate.dtype), sems],
    )


def solution(mesh):
    axes = ("z_lo", "y", "z_hi", "x", "core")
    fine = Mesh(mesh.devices.reshape(4, 4, 4, 4, 2), axes)
    placed = P(axes[:2], axes[2:])
    return jax.shard_map(
        shards, mesh=fine, in_specs=(placed,), out_specs=placed, check_vma=False
    )
```

```python
import math

import jax
import jax.numpy as jnp
from jax import lax
from jax.experimental import pallas as pl
from jax.experimental.pallas import tpu as pltpu
from jax.sharding import Mesh
from jax.sharding import PartitionSpec as P

D = 3584
FF = 18432

coef_linear = 3.4445
coef_cubic = -4.775
coef_quintic = 2.0315

LANES = 128
PAIRS = [[0, 2], [4, 6], [3, 5], [7, 1]], [[2, 4], [6, 0], [1, 3], [5, 7]]
VMEM = pl.BlockSpec(memory_space=pltpu.VMEM)
SMEM = pl.BlockSpec(memory_space=pltpu.SMEM)
HBM = pl.BlockSpec(memory_space=pltpu.HBM)
ANY = pl.BlockSpec(memory_space=pl.ANY)


def call(kernel, operands, output, spec=VMEM, scratch=(), flops=0):
    arrays, in_specs = zip(*operands)
    return pl.pallas_call(
        kernel,
        out_shape=output,
        in_specs=in_specs,
        out_specs=spec,
        scratch_shapes=scratch,
        compiler_params=pltpu.CompilerParams(vmem_limit_bytes=16 * 1024 * 1024),
        cost_estimate=pl.CostEstimate(
            flops=flops,
            bytes_accessed=2 * sum(math.prod(array.shape) for array in arrays),
            transcendentals=0,
        ),
    )(*arrays)


def bf16(*shape):
    return jax.ShapeDtypeStruct(shape, jnp.bfloat16)


def dot(lhs, rhs, rhs_dim):
    return lax.dot_general(
        lhs, rhs, (((1,), (rhs_dim,)), ((), ())), preferred_element_type=jnp.float32
    )


def pieces(rows, cols):
    whole, rest = cols // LANES, cols % LANES
    for k in range(whole):
        yield slice(0, rows), slice(k * LANES, (k + 1) * LANES), slice(k * rows, (k + 1) * rows), slice(0, LANES)
    each = rows * rest // LANES
    for k in range(LANES // rest if rest else 0):
        columns = slice(k * rest, (k + 1) * rest)
        yield slice(k * each, (k + 1) * each), slice(whole * LANES, cols), slice(whole * rows, whole * rows + each), columns


def unpack(packed, out):
    rows = out.shape[0] // packed.shape[0]
    for i in range(packed.shape[0]):
        for row, col, packed_row, packed_col in pieces(rows, out.shape[1]):
            row = slice(i * rows + row.start, i * rows + row.stop)
            out[row, col] = packed[i, packed_row, packed_col]


def first_kernel(array, out, packed, sems):
    copies = [pltpu.make_async_copy(array, out.at[i], sems.at[i]) for i in range(out.shape[0])]
    for copy in copies:
        copy.start()
    for row, col, packed_row, packed_col in pieces(*array.shape):
        packed[packed_row, packed_col] = array[row, col]
    for copy in copies:
        copy.wait()


def gram_kernel(left, right, out, held):
    blocks, cores, rows, cols = left.shape
    whole = cols - cols % LANES
    size = held.shape[0] // blocks
    for i in range(blocks):
        for k in range(cores):
            for row, col, packed_row, packed_col in pieces(size, cols):
                start = k * whole + col.start
                if col.start >= whole:
                    start = cores * whole + k * (cols - whole)
                place = slice(start, start + col.stop - col.start)
                row = slice(i * size + row.start, i * size + row.stop)
                held[row, place] = right[i, k, packed_row, packed_col]
    lhs = [left[:, k, :, :whole] for k in range(cores)]
    lhs = jnp.concatenate(lhs + [left[:, k, :, whole:] for k in range(cores)], axis=-1)
    tile = dot(lhs.reshape(blocks * rows, cores * cols), held[...], 1)
    out[...] = tile.astype(out.dtype).reshape(out.shape)


def own_kernel(core, right, out):
    out[...] = right[:, pl.ds(core[0], 1)].reshape(out.shape)


def product_kernel(left, right, out, held):
    unpack(right, held)
    product = dot(left[...], held[...], 0).astype(out.dtype)
    rows = product.shape[0] // out.shape[0]
    for i in range(out.shape[0]):
        block = product[i * rows : (i + 1) * rows]
        for row, col, packed_row, packed_col in pieces(rows, product.shape[1]):
            out[i, packed_row, packed_col] = block[row, col]


def update_kernel(iterate, once, parts, out, held, sem):
    fetch = pltpu.make_async_copy(iterate, held, sem)
    fetch.start()
    packed = coef_cubic * once[...]
    packed += coef_quintic * jnp.sum(parts[...].astype(jnp.float32), axis=0)
    fetch.wait()
    for row, col, packed_row, packed_col in pieces(*out.shape):
        step = coef_linear * held[row, col].astype(jnp.float32) + packed[packed_row, packed_col]
        out[row, col] = (0.2 * math.sqrt(max(D, FF)) * step).astype(out.dtype)


def total(parts):
    return jnp.sum(parts.astype(jnp.float32), axis=0)


def gather(array, axes):
    return lax.all_gather(array.astype(jnp.float16), axes, axis=0).astype(jnp.bfloat16)


def exchange(array, axes):
    return lax.all_to_all(array, axes, 0, 0, tiled=True)


def shards(iterate):
    rows, cols = iterate.shape
    half = rows // 2
    core = lax.axis_index("core").astype(jnp.int32).reshape(1)
    sems = pltpu.SemaphoreType.DMA

    packed = rows * cols // LANES
    left, right = call(
        first_kernel,
        [(iterate, VMEM)],
        (bf16(4, rows, cols), bf16(packed, LANES)),
        spec=(HBM, VMEM),
        scratch=[sems((4,))],
    )
    left = exchange(left.reshape(8, half, cols), ("y", "core")).reshape(4, 2, half, cols)
    right = gather(right, ("z_lo", "core")).reshape(4, 2, packed, LANES)

    tile = call(
        gram_kernel,
        [(left, VMEM), (right, VMEM)],
        bf16(4, half, 4 * rows),
        scratch=[pltpu.VMEM((4 * rows, 2 * cols), jnp.bfloat16)],
        flops=4 * 4 * half * 4 * rows * cols,
    )
    tile, right = lax.optimization_barrier((tile, right))
    own = call(own_kernel, [(core, SMEM), (right, VMEM)], bf16(4, packed, LANES))
    tile, own = lax.optimization_barrier((tile, own))
    piece = total(exchange(tile, "x"))
    for groups in PAIRS:
        piece = piece.astype(jnp.float16)
        piece = total(lax.all_gather(piece, ("z_hi", "core"), axis=0, axis_index_groups=groups))
    gram = gather(piece, ("x", "core")).reshape(4 * rows, 4 * rows)

    def gram_times(array):
        parts = call(
            product_kernel,
            [(gram, VMEM), (array, VMEM)],
            bf16(4, packed, LANES),
            scratch=[pltpu.VMEM((4 * rows, cols), jnp.bfloat16)],
            flops=2 * gram.size * cols,
        )
        return exchange(parts, "y")

    once = total(gram_times(own))
    twice = gram_times(lax.all_gather(once.astype(jnp.bfloat16), "z_lo", axis=0))
    return call(
        update_kernel,
        [(iterate, ANY), (once, VMEM), (twice, VMEM)],
        bf16(rows, cols),
        scratch=[pltpu.VMEM(iterate.shape, iterate.dtype), sems],
    )


def solution(mesh):
    axes = ("z_lo", "y", "z_hi", "x", "core")
    fine = Mesh(mesh.devices.reshape(4, 4, 4, 4, 2), axes)
    placed = P(axes[:2], axes[2:])
    return jax.shard_map(
        shards, mesh=fine, in_specs=(placed,), out_specs=placed, check_vma=False
    )
```

```python
import math

import jax
import jax.numpy as jnp
from jax import lax
from jax.experimental import pallas as pl
from jax.experimental.pallas import tpu as pltpu
from jax.sharding import Mesh
from jax.sharding import PartitionSpec as P

D = 3584
FF = 18432

coef_linear = 3.4445
coef_cubic = -4.775
coef_quintic = 2.0315

LANES = 128
PAIRS = [[0, 2], [4, 6], [3, 5], [7, 1]], [[2, 4], [6, 0], [1, 3], [5, 7]]
VMEM = pl.BlockSpec(memory_space=pltpu.VMEM)
SMEM = pl.BlockSpec(memory_space=pltpu.SMEM)
HBM = pl.BlockSpec(memory_space=pltpu.HBM)
ANY = pl.BlockSpec(memory_space=pl.ANY)


def call(kernel, operands, output, spec=VMEM, scratch=(), flops=0):
    arrays, in_specs = zip(*operands)
    return pl.pallas_call(
        kernel,
        out_shape=output,
        in_specs=in_specs,
        out_specs=spec,
        scratch_shapes=scratch,
        compiler_params=pltpu.CompilerParams(vmem_limit_bytes=16 * 1024 * 1024),
        cost_estimate=pl.CostEstimate(
            flops=flops,
            bytes_accessed=2 * sum(math.prod(array.shape) for array in arrays),
            transcendentals=0,
        ),
    )(*arrays)


def bf16(*shape):
    return jax.ShapeDtypeStruct(shape, jnp.bfloat16)


def dot(lhs, rhs, rhs_dim):
    return lax.dot_general(
        lhs, rhs, (((1,), (rhs_dim,)), ((), ())), preferred_element_type=jnp.float32
    )


def pieces(rows, cols):
    whole, rest = cols // LANES, cols % LANES
    for k in range(whole):
        yield slice(0, rows), slice(k * LANES, (k + 1) * LANES), slice(k * rows, (k + 1) * rows), slice(0, LANES)
    each = rows * rest // LANES
    for k in range(LANES // rest if rest else 0):
        columns = slice(k * rest, (k + 1) * rest)
        yield slice(k * each, (k + 1) * each), slice(whole * LANES, cols), slice(whole * rows, whole * rows + each), columns


def unpack(packed, out):
    rows = out.shape[0] // packed.shape[0]
    for i in range(packed.shape[0]):
        for row, col, packed_row, packed_col in pieces(rows, out.shape[1]):
            row = slice(i * rows + row.start, i * rows + row.stop)
            out[row, col] = packed[i, packed_row, packed_col]


def first_kernel(array, out, packed, sems):
    copies = [pltpu.make_async_copy(array, out.at[i], sems.at[i]) for i in range(out.shape[0])]
    for copy in copies:
        copy.start()
    for row, col, packed_row, packed_col in pieces(*array.shape):
        packed[packed_row, packed_col] = array[row, col]
    for copy in copies:
        copy.wait()


def gram_kernel(left, right, out, held):
    blocks, cores, rows, cols = left.shape
    whole = cols - cols % LANES
    size = held.shape[0] // blocks
    for i in range(blocks):
        for k in range(cores):
            for row, col, packed_row, packed_col in pieces(size, cols):
                start = k * whole + col.start
                if col.start >= whole:
                    start = cores * whole + k * (cols - whole)
                place = slice(start, start + col.stop - col.start)
                row = slice(i * size + row.start, i * size + row.stop)
                held[row, place] = right[i, k, packed_row, packed_col]
    lhs = [left[:, k, :, :whole] for k in range(cores)]
    lhs = jnp.concatenate(lhs + [left[:, k, :, whole:] for k in range(cores)], axis=-1)
    tile = dot(lhs.reshape(blocks * rows, cores * cols), held[...], 1)
    out[...] = tile.astype(out.dtype).reshape(out.shape)


def own_product_kernel(core, left, right, out, held):
    product_kernel(left, right.at[:, core[0]], out, held)


def product_kernel(left, right, out, held):
    unpack(right, held)
    product = dot(left[...], held[...], 0).astype(out.dtype)
    rows = product.shape[0] // out.shape[0]
    for i in range(out.shape[0]):
        block = product[i * rows : (i + 1) * rows]
        for row, col, packed_row, packed_col in pieces(rows, product.shape[1]):
            out[i, packed_row, packed_col] = block[row, col]


def update_kernel(iterate, once, parts, out, held, sem):
    fetch = pltpu.make_async_copy(iterate, held, sem)
    fetch.start()
    packed = coef_cubic * once[...]
    packed += coef_quintic * jnp.sum(parts[...].astype(jnp.float32), axis=0)
    fetch.wait()
    for row, col, packed_row, packed_col in pieces(*out.shape):
        step = coef_linear * held[row, col].astype(jnp.float32) + packed[packed_row, packed_col]
        out[row, col] = (0.2 * math.sqrt(max(D, FF)) * step).astype(out.dtype)


def total(parts):
    return jnp.sum(parts.astype(jnp.float32), axis=0)


def gather(array, axes):
    return lax.all_gather(array.astype(jnp.float16), axes, axis=0).astype(jnp.bfloat16)


def exchange(array, axes):
    return lax.all_to_all(array, axes, 0, 0, tiled=True)


def shards(iterate):
    rows, cols = iterate.shape
    half = rows // 2
    core = lax.axis_index("core").astype(jnp.int32).reshape(1)
    sems = pltpu.SemaphoreType.DMA

    packed = rows * cols // LANES
    left, right = call(
        first_kernel,
        [(iterate, VMEM)],
        (bf16(4, rows, cols), bf16(packed, LANES)),
        spec=(HBM, VMEM),
        scratch=[sems((4,))],
    )
    left = exchange(left.reshape(8, half, cols), ("y", "core")).reshape(4, 2, half, cols)
    right = gather(right, ("z_lo", "core")).reshape(4, 2, packed, LANES)

    tile = call(
        gram_kernel,
        [(left, VMEM), (right, VMEM)],
        bf16(4, half, 4 * rows),
        scratch=[pltpu.VMEM((4 * rows, 2 * cols), jnp.bfloat16)],
        flops=4 * 4 * half * 4 * rows * cols,
    )
    piece = total(exchange(tile, "x"))
    for groups in PAIRS:
        piece = piece.astype(jnp.float16)
        piece = total(lax.all_gather(piece, ("z_hi", "core"), axis=0, axis_index_groups=groups))
    gram = gather(piece, ("x", "core")).reshape(4 * rows, 4 * rows)

    def gram_times(kernel, *operands):
        parts = call(
            kernel,
            operands,
            bf16(4, packed, LANES),
            scratch=[pltpu.VMEM((4 * rows, cols), jnp.bfloat16)],
            flops=2 * gram.size * cols,
        )
        return exchange(parts, "y")

    once = total(
        gram_times(own_product_kernel, (core, SMEM), (gram, VMEM), (right, VMEM))
    )
    twice = lax.all_gather(once.astype(jnp.bfloat16), "z_lo", axis=0)
    twice = gram_times(product_kernel, (gram, VMEM), (twice, VMEM))
    return call(
        update_kernel,
        [(iterate, ANY), (once, VMEM), (twice, VMEM)],
        bf16(rows, cols),
        scratch=[pltpu.VMEM(iterate.shape, iterate.dtype), sems],
    )


def solution(mesh):
    axes = ("z_lo", "y", "z_hi", "x", "core")
    fine = Mesh(mesh.devices.reshape(4, 4, 4, 4, 2), axes)
    placed = P(axes[:2], axes[2:])
    return jax.shard_map(
        shards, mesh=fine, in_specs=(placed,), out_specs=placed, check_vma=False
    )
```
